128 devices in a mesh: dom: 8 (over z, x_lo), feat: 16 (over y, x_hi, core).
Axes of the slice: x: 4 (x_hi: 2, x_lo: 2; x = x_hi * 2 + x_lo), y: 4, z: 4, core: 2. Of those that a mesh axis runs over, the one named last changes fastest.
Arguments:
- particles: bfloat16 [832, 196608], P('dom', 'feat'), may hold values from -13 to 13
- gradients: bfloat16 [832, 196608], P('dom', 'feat'), may hold values from -6 to 6
- spread: float32 [1], replicated, may hold values from 1 to 2
Outputs:
- drive: float32 [832, 196608], P('dom', 'feat')
- repel: float32 [832, 196608], P('dom', 'feat')
The draws below stay inside these ranges and needn't reach their ends.
All inputs are finite; a program needn't handle non-finite values.
Results may differ from the reference program's by a relative error of at most 0.0028.
Values may be sent and summed in bfloat16 or wider, within the bound.
A program may use at most 128 MiB of HBM per device.

```python
import jax
import jax.numpy as jnp

DIMS = 196608
PARTICLES = 832


def draw_particles(key, part):
    key = jax.random.fold_in(key, 7)
    first, second, third = jax.random.split(key, 3)
    latent = jax.random.uniform(first, (PARTICLES, 4), jnp.float32, -2.0, 2.0)
    heading = jnp.clip(jax.random.normal(second, (DIMS,), jnp.float32), -4.0, 4.0)
    noise = jnp.clip(jax.random.normal(third, (PARTICLES, DIMS), jnp.float32), -5.0, 5.0)
    classes = jnp.arange(DIMS) % 4
    picked = jnp.take(latent, classes, axis=1)
    return (noise + picked * heading[None, :]).astype(jnp.bfloat16)


def shard_levels(rng, shape, pieces, least, high):
    level, own = 1.0, jax.random.fold_in(rng, 6)
    for dim, parts in pieces:
        heights = jnp.exp(jax.random.uniform(jax.random.fold_in(own, dim), (parts,), jnp.float32, least / len(pieces), high / len(pieces)))
        level = level * jnp.repeat(heights, shape[dim] // parts).reshape([-1 if axis == dim else 1 for axis in range(len(shape))])
    return level


def gaussian(rng, extent, scale, bound, cuts=(), dtype=jnp.bfloat16):
    level = shard_levels(rng, extent, cuts, -0.22, 0.18) if cuts else 1.0
    values = jax.random.normal(rng, extent, jnp.float32) * scale * level
    return jnp.minimum(jnp.maximum(values, -bound), bound).astype(dtype)


def setup_inputs(seed: int = 0) -> dict:
    key_list = jax.random.split(jax.random.key(seed), 4)
    particles = draw_particles(jax.random.fold_in(key_list[3], 71), 0)
    gradients = gaussian(key_list[1], (PARTICLES, DIMS), 1.0, 6.0, ((0, 8), (1, 16)))
    spread = jnp.clip(jax.random.uniform(key_list[2], (1,), jnp.float32, 1.0, 2.0), 1.0, 2.0)
    return {"particles": particles, "gradients": gradients, "spread": spread}


def reference(particles, gradients, spread):
    wide = particles.astype(jnp.float32)
    squares = jnp.sum(wide * wide, axis=1)
    inner = jnp.dot(particles, particles.T, preferred_element_type=jnp.float32)
    dist = squares[:, None] + squares[None, :] - 2.0 * inner
    kern = jnp.exp(-dist / (DIMS * spread[0])).astype(jnp.bfloat16)
    totals = jnp.sum(kern.astype(jnp.float32), axis=1)
    drive = jnp.dot(kern, gradients, preferred_element_type=jnp.float32)
    pulled = jnp.dot(kern, particles, preferred_element_type=jnp.float32)
    repel = totals[:, None] * wide - pulled
    return drive, repel
```

```python
import jax
import jax.numpy as jnp
from jax import lax
from jax.experimental import pallas as pl
from jax.experimental.pallas import tpu as pltpu
from jax.sharding import PartitionSpec as P

DIMS = 196608
ROWS = 104
COLS = 12288
BLOCKS = 8
WIDTH = COLS // BLOCKS
PAIR = 2 * ROWS
FLAT = 4096
HALF, QUARTER, CHUNK = FLAT // 2, FLAT // 8, FLAT // 128
MESH = pl.DeviceIdType.MESH


def row_of_block(k, i):
    return pl.multiple_of((BLOCKS * k + i) * ROWS, 8)


def kernel(
    x, g, spread, drive_out, repel_out,
    xt, gt, own_gram, sq_col, sq_row, part, from_core, half_sum, half_wire, from_y, quarter_sum, from_zx,
    kern, kern_wide, kern_rows, drive_stage, repel_stage,
    x_send, x_recv, g_send, g_recv, d_send, d_recv, r_send, r_recv, own_sem,
    c_send, c_recv, y_send, y_recv, p_send, p_recv, ap_send, ap_recv, ay_send, ay_recv, ac_send, ac_recv,
):
    dom, feat = lax.axis_index("dom"), lax.axis_index("feat")
    z, x_lo = dom // 2, dom % 2
    y, x_hi, core = feat // 4, (feat // 2) % 2, feat % 2
    xx = x_hi * 2 + x_lo

    def dom_peer(r):
        return (z + r // 2) % 4 * 2 + (x_lo + r % 2) % 2

    def plane_peer(r):
        z2, x2 = (z + r // 4) % 4, (xx + r % 4) % 4
        return z2 * 4 + x2, (z2 * 2 + x2 % 2, y * 4 + x2 // 2 * 2 + core)

    def y_peer(r):
        y2 = (y + r) % 4
        return y2, (dom, y2 * 4 + x_hi * 2 + core)

    sibling = (dom, y * 4 + x_hi * 2 + 1 - core)

    barrier = pltpu.get_barrier_semaphore()

    @pl.loop(1, 16)
    def _(r):
        pl.semaphore_signal(barrier, inc=1, device_id=plane_peer(r)[1], device_id_type=MESH)

    @pl.loop(1, 4)
    def _(r):
        pl.semaphore_signal(barrier, inc=1, device_id=y_peer(r)[1], device_id_type=MESH)

    pl.semaphore_signal(barrier, inc=1, device_id=sibling, device_id_type=MESH)
    pl.semaphore_wait(barrier, 19)

    def columns(block):
        return pl.ds(pl.multiple_of(block * WIDTH, 128), WIDTH)

    def inward(src, dst, send, recv, r):
        to = dom_peer(r)
        return pltpu.make_async_remote_copy(
            src_ref=src.at[:, columns(to)], dst_ref=dst.at[dom], send_sem=send.at[r], recv_sem=recv.at[r],
            device_id=(to, feat), device_id_type=MESH)

    def outward(src, dst, send, recv, r):
        to = dom_peer(r)
        return pltpu.make_async_remote_copy(
            src_ref=src.at[to], dst_ref=dst.at[:, columns(dom)], send_sem=send.at[r], recv_sem=recv.at[r],
            device_id=(to, feat), device_id_type=MESH)

    own_x = pltpu.make_async_copy(x.at[:, columns(dom)], xt.at[dom], own_sem.at[0])
    own_g = pltpu.make_async_copy(g.at[:, columns(dom)], gt.at[dom], own_sem.at[1])

    @pl.loop(1, BLOCKS)
    def _(r):
        inward(x, xt, x_send, x_recv, r).start()

    own_x.start()
    own_g.start()
    part[...] = jnp.zeros_like(part)

    @pl.loop(1, BLOCKS)
    def _(r):
        inward(x, xt, x_send, x_recv, r).wait_send()
        inward(g, gt, g_send, g_recv, r).start()

    own_x.wait()

    @pl.loop(1, BLOCKS)
    def _(r):
        inward(x, xt, x_send, x_recv, r).wait_recv()

    def gram(i, j):
        return lax.dot_general(xt[i], xt[j], (((1,), (1,)), ((), ())), preferred_element_type=jnp.float32)

    on_diagonal = lax.broadcasted_iota(jnp.int32, (ROWS, ROWS), 0) == lax.broadcasted_iota(jnp.int32, (ROWS, ROWS), 1)

    @pl.loop(0, BLOCKS)
    def _(i):
        block = gram(i, i)
        own_gram[i] = block
        picked = jnp.where(on_diagonal, block, 0.0)
        sq_col[i] = jnp.sum(picked, axis=1, keepdims=True)
        sq_row[i] = jnp.sum(picked, axis=0, keepdims=True)

    def partial_dist(k, i):
        j = (i + k) % BLOCKS
        inner = own_gram[i] if k == 0 else gram(i, j)
        return sq_col[i] + sq_row[j] - 2.0 * inner

    def store_pair(k, q):
        both = jnp.concatenate([partial_dist(k, 2 * q), partial_dist(k, 2 * q + 1)], axis=0)
        part[pl.ds(pl.multiple_of((4 * k + q) * PAIR, 16), PAIR), 0:ROWS] = both.astype(jnp.bfloat16)

    @pl.loop(0, 4)
    def _(q):
        for k in range(4):
            store_pair(k, q)

    @pl.loop(0, 2)
    def _(q):
        store_pair(4, q)

    def half_rows(which):
        return pl.ds(pl.multiple_of(which * HALF, 16), HALF)

    to_core = pltpu.make_async_remote_copy(
        src_ref=part.at[half_rows(1 - core)], dst_ref=from_core, send_sem=c_send, recv_sem=c_recv,
        device_id=sibling, device_id_type=MESH)
    to_core.start()
    to_core.wait()
    half_sum[...] = part[half_rows(core)].astype(jnp.float32) + from_core[...].astype(jnp.float32)
    half_wire[...] = half_sum[...].astype(jnp.bfloat16)

    def to_y(r):
        y2, device = y_peer(r)
        return pltpu.make_async_remote_copy(
            src_ref=half_wire.at[pl.ds(pl.multiple_of(y2 * QUARTER, 16), QUARTER)], dst_ref=from_y.at[r],
            send_sem=y_send.at[r], recv_sem=y_recv.at[r], device_id=device, device_id_type=MESH)

    for r in range(1, 4):
        to_y(r).start()
    total = half_sum[pl.ds(pl.multiple_of(y * QUARTER, 16), QUARTER)]
    for r in range(1, 4):
        to_y(r).wait()
    for r in range(1, 4):
        total = total + from_y[r].astype(jnp.float32)
    quarter_sum[...] = total

    member = z * 4 + xx

    def to_plane(r):
        m2, device = plane_peer(r)
        return pltpu.make_async_remote_copy(
            src_ref=quarter_sum.at[pl.ds(pl.multiple_of(m2 * CHUNK, 8), CHUNK)], dst_ref=from_zx.at[r],
            send_sem=p_send.at[r], recv_sem=p_recv.at[r], device_id=device, device_id_type=MESH)

    @pl.loop(1, 16)
    def _(r):
        to_plane(r).start()

    from_zx[0] = quarter_sum[pl.ds(pl.multiple_of(member * CHUNK, 8), CHUNK)]

    @pl.loop(1, 16)
    def _(r):
        to_plane(r).wait()

    dist = jnp.sum(from_zx[...], axis=0)
    width = DIMS * spread[0]
    base = pl.multiple_of(core * HALF + y * QUARTER, 16)
    mine = pl.ds(pl.multiple_of(base + member * CHUNK, 16), CHUNK)
    kern[mine] = jnp.exp(-dist / width).astype(jnp.bfloat16)

    def kern_to_plane(r):
        return pltpu.make_async_remote_copy(
            src_ref=kern.at[mine], dst_ref=kern.at[mine], send_sem=ap_send.at[r], recv_sem=ap_recv.at[r],
            device_id=plane_peer(r)[1], device_id_type=MESH)

    @pl.loop(1, 16)
    def _(r):
        kern_to_plane(r).start()

    @pl.loop(1, 16)
    def _(r):
        kern_to_plane(r).wait()

    quarter = pl.ds(base, QUARTER)

    def kern_to_y(r):
        return pltpu.make_async_remote_copy(
            src_ref=kern.at[quarter], dst_ref=kern.at[quarter], send_sem=ay_send.at[r], recv_sem=ay_recv.at[r],
            device_id=y_peer(r)[1], device_id_type=MESH)

    def kern_to_core(r):
        y2 = (y + 4 - r) % 4
        rows = pl.ds(pl.multiple_of(core * HALF + y2 * QUARTER, 16), QUARTER)
        return pltpu.make_async_remote_copy(
            src_ref=kern.at[rows], dst_ref=kern.at[rows], send_sem=ac_send.at[r], recv_sem=ac_recv.at[r],
            device_id=sibling, device_id_type=MESH)

    for r in range(1, 4):
        kern_to_y(r).start()
    kern_to_core(0).start()
    for r in range(1, 4):
        kern_to_y(r).wait_recv()
        kern_to_core(r).start()
    for r in range(4):
        kern_to_core(r).wait()
    for r in range(1, 4):
        kern_to_y(r).wait_send()
    kern_wide[...] = kern[...].astype(jnp.float32)

    def block(k, i):
        return kern_wide[pl.ds(row_of_block(k, i), ROWS), 0:ROWS]

    def kern_block(i, k):
        j = (i + k) % BLOCKS
        if k < 4:
            return block(k, i)
        if k > 4:
            return block(BLOCKS - k, j).T
        across = block(4, i % 4)
        return jnp.where(i < 4, across, across.T)

    @pl.loop(1, BLOCKS + 1)
    def _(step):
        r = step % BLOCKS
        i = dom_peer(r)
        totals = jnp.zeros((ROWS, 1), jnp.float32)
        pulled = jnp.zeros((ROWS, WIDTH), jnp.float32)
        for k in range(BLOCKS):
            wide = kern_block(i, k)
            totals = totals + jnp.sum(wide, axis=1, keepdims=True)
            narrow = wide.astype(jnp.bfloat16)
            kern_rows[i, k] = narrow
            pulled = pulled + jnp.dot(narrow, xt[(i + k) % BLOCKS], preferred_element_type=jnp.float32)
        repel_stage[i] = (totals * xt[i].astype(jnp.float32) - pulled).astype(jnp.bfloat16)

        @pl.when(step < BLOCKS)
        def _():
            outward(repel_stage, repel_out, r_send, r_recv, r).start()

    own_g.wait()

    @pl.loop(1, BLOCKS)
    def _(r):
        inward(g, gt, g_send, g_recv, r).wait()

    @pl.loop(1, BLOCKS + 1)
    def _(step):
        r = step % BLOCKS
        i = dom_peer(r)
        driven = jnp.zeros((ROWS, WIDTH), jnp.float32)
        for k in range(BLOCKS):
            driven = driven + jnp.dot(kern_rows[i, k], gt[(i + k) % BLOCKS], preferred_element_type=jnp.float32)
        drive_stage[i] = driven.astype(jnp.bfloat16)

        @pl.when(step < BLOCKS)
        def _():
            outward(drive_stage, drive_out, d_send, d_recv, r).start()

    own_r = pltpu.make_async_copy(repel_stage.at[dom], repel_out.at[:, columns(dom)], own_sem.at[0])
    own_d = pltpu.make_async_copy(drive_stage.at[dom], drive_out.at[:, columns(dom)], own_sem.at[1])
    own_r.start()
    own_d.start()
    own_r.wait()
    own_d.wait()

    @pl.loop(1, BLOCKS)
    def _(r):
        outward(repel_stage, repel_out, r_send, r_recv, r).wait()

    @pl.loop(1, BLOCKS)
    def _(r):
        outward(drive_stage, drive_out, d_send, d_recv, r).wait()


def per_device(particles, gradients, spread):
    bf16, f32 = jnp.bfloat16, jnp.float32
    vmem, dma = pltpu.VMEM, pltpu.SemaphoreType.DMA
    slab = (BLOCKS, ROWS, WIDTH)
    drive, repel = pl.pallas_call(
        kernel,
        out_shape=[jax.ShapeDtypeStruct((ROWS, COLS), bf16)] * 2,
        in_specs=[pl.BlockSpec(memory_space=pl.ANY)] * 2 + [pl.BlockSpec(memory_space=pltpu.SMEM)],
        out_specs=[pl.BlockSpec(memory_space=pl.ANY)] * 2,
        scratch_shapes=[
            vmem(slab, bf16), vmem(slab, bf16),
            vmem((BLOCKS, ROWS, ROWS), f32), vmem((BLOCKS, ROWS, 1), f32), vmem((BLOCKS, 1, ROWS), f32),
            vmem((FLAT, 128), bf16), vmem((HALF, 128), bf16), vmem((HALF, 128), f32), vmem((HALF, 128), bf16),
            vmem((4, QUARTER, 128), bf16), vmem((QUARTER, 128), f32), vmem((16, CHUNK, 128), f32),
            vmem((FLAT, 128), bf16), vmem((FLAT, 128), f32), vmem((BLOCKS, BLOCKS, ROWS, ROWS), bf16),
            vmem(slab, bf16), vmem(slab, bf16),
        ]
        + [dma((BLOCKS,))] * 8 + [dma((2,))]
        + [dma(()), dma(()), dma((4,)), dma((4,)), dma((16,)), dma((16,))]
        + [dma((16,)), dma((16,)), dma((4,)), dma((4,)), dma((4,)), dma((4,))],
        compiler_params=pltpu.CompilerParams(
            collective_id=0, has_side_effects=True, vmem_limit_bytes=56 * 2**20),
        name="svgd",
    )(particles, gradients, spread)
    return drive.astype(f32), repel.astype(f32)


def solution(mesh):
    return jax.shard_map(
        per_device,
        mesh=mesh,
        in_specs=(P("dom", "feat"), P("dom", "feat"), P()),
        out_specs=(P("dom", "feat"), P("dom", "feat")),
        check_vma=False,
    )
```

```python
import jax
import jax.numpy as jnp
from jax import lax
from jax.experimental import pallas as pl
from jax.experimental.pallas import tpu as pltpu
from jax.sharding import PartitionSpec as P

DIMS = 196608
ROWS = 104
PAD_K, PAD_M = 128, 112
COLS = 12288
BLOCKS = 8
PIECES = 3
WIDTH = COLS // BLOCKS
PIECE = WIDTH // PIECES
G_PIECES = 6
G_PIECE = WIDTH // G_PIECES
G_AT = (1, 0, 1, 1, 1, 2)
PARTS = 2
FLAT = 4096
PART = FLAT // PARTS
HALF, QUARTER, CHUNK = PART // 2, PART // 8, PART // 128
SUPER = [(i, i) for i in range(4)] + [(i, j) for i in range(4) for j in range(i + 1, 4)]
PAIRS = []
for n, (si, sj) in enumerate(SUPER):
    for a in range(2):
        for b in range(2):
            if 2 * si + a <= 2 * sj + b:
                PAIRS.append((2 * si + a, 2 * sj + b, n, a * PAD_K, b * PAD_K))
FIRST = [n for n in range(len(PAIRS)) if (n + 1) * ROWS <= PART]
MESH = pl.DeviceIdType.MESH


def kernel(
    x, g, spread, drive_out, repel_out,
    xt, gt, xd, gd, acc, part, part_wire, from_core, core_sum, core_wire, from_y, y_sum, from_zx,
    kern, kern_wide, full, totals, product, drive_stage, repel_stage, drive_land, repel_land,
    x_send, x_recv, g_send, g_recv, d_send, d_recv, r_send, r_recv, own_sem,
    c_send, c_recv, y_send, y_recv, p_send, p_recv, ap_send, ap_recv, ay_send, ay_recv, ac_send, ac_recv,
):
    f32, bf16 = jnp.float32, jnp.bfloat16
    dom, feat = lax.axis_index("dom"), lax.axis_index("feat")
    z, x_lo = dom // 2, dom % 2
    y, x_hi, core = feat // 4, (feat // 2) % 2, feat % 2
    xx = x_hi * 2 + x_lo
    member = z * 4 + xx

    def dom_peer(r):
        return (z + r // 2) % 4 * 2 + (x_lo + r % 2) % 2

    def plane_peer(r):
        z2, x2 = (z + r // 4) % 4, (xx + r % 4) % 4
        return z2 * 4 + x2, (z2 * 2 + x2 % 2, y * 4 + x2 // 2 * 2 + core)

    def y_peer(r):
        y2 = (y + r) % 4
        return y2, (dom, y2 * 4 + x_hi * 2 + core)

    sibling = (dom, y * 4 + x_hi * 2 + 1 - core)

    barrier = pltpu.get_barrier_semaphore()

    @pl.loop(1, 16)
    def _(r):
        pl.semaphore_signal(barrier, inc=1, device_id=plane_peer(r)[1], device_id_type=MESH)

    @pl.loop(1, 4)
    def _(r):
        pl.semaphore_signal(barrier, inc=1, device_id=y_peer(r)[1], device_id_type=MESH)

    pl.semaphore_signal(barrier, inc=1, device_id=sibling, device_id_type=MESH)
    pl.semaphore_wait(barrier, 19)

    def columns(block, c):
        return pl.ds(pl.multiple_of(block * WIDTH + c * PIECE, 128), PIECE)

    def remote(src, dst, send, recv, device):
        return pltpu.make_async_remote_copy(
            src_ref=src, dst_ref=dst, send_sem=send, recv_sem=recv, device_id=device, device_id_type=MESH)

    def inward(src, dst, send, recv, c, r):
        to = dom_peer(r)
        return remote(src.at[:, columns(to, c)], dst.at[c, dom], send.at[c, r], recv.at[c, r], (to, feat))

    def x_in(c, r):
        return inward(x, xt, x_send, x_recv, c, r)

    def g_in(p, r):
        to, lane = dom_peer(r), p % 2 * G_PIECE
        source = g.at[:, pl.ds(pl.multiple_of(to * WIDTH + p * G_PIECE, 128), G_PIECE)]
        target = gt.at[p // 2, dom, :, pl.ds(lane, G_PIECE)]
        return remote(source, target, g_send.at[p, r], g_recv.at[p, r], (to, feat))

    def start_g(point):
        for p in range(sum(G_AT[:point]), sum(G_AT[: point + 1])):
            @pl.loop(1, BLOCKS)
            def _(r):
                g_in(p, r).start()

    def own_copy(src, dst, which, c):
        return pltpu.make_async_copy(src.at[:, columns(dom, c)], dst.at[c, dom], own_sem.at[which, c])

    for c in range(2):
        @pl.loop(1, BLOCKS)
        def _(r):
            x_in(c, r).start()

    for c in range(PIECES):
        own_copy(x, xt, 0, c).start()
    for c in range(PIECES):
        own_copy(g, gt, 1, c).start()
    part[...] = jnp.zeros_like(part)
    acc[...] = jnp.zeros_like(acc)
    xd[...] = jnp.zeros_like(xd)
    gd[...] = jnp.zeros_like(gd)
    full[...] = jnp.zeros_like(full)

    def spread_out(src, dst, c):
        for b in range(BLOCKS):
            dst[c, b * PAD_K : b * PAD_K + ROWS] = src[c, b]

    for c in range(PIECES):
        @pl.loop(1, BLOCKS)
        def _(r):
            x_in(c, r).wait_send()
            if c == 0:
                x_in(2, r).start()

        if c > 0:
            start_g(c - 1)
        own_copy(x, xt, 0, c).wait()

        @pl.loop(1, BLOCKS)
        def _(r):
            x_in(c, r).wait_recv()

        spread_out(xt, xd, c)
        for n, (si, sj) in enumerate(SUPER):
            left = xd[c, si * 2 * PAD_K : (si + 1) * 2 * PAD_K]
            right = xd[c, sj * 2 * PAD_K : (sj + 1) * 2 * PAD_K]
            acc[n] += lax.dot_general(left, right, (((1,), (1,)), ((), ())), preferred_element_type=f32)

    size = (2 * PAD_K, 2 * PAD_K)
    on_diagonal = lax.broadcasted_iota(jnp.int32, size, 0) == lax.broadcasted_iota(jnp.int32, size, 1)
    sq_col, sq_row = [], []
    for n in range(4):
        picked = jnp.where(on_diagonal, acc[n], 0.0)
        col, row = jnp.sum(picked, axis=1, keepdims=True), jnp.sum(picked, axis=0, keepdims=True)
        for a in (0, PAD_K):
            sq_col.append(col[a : a + ROWS])
            sq_row.append(row[:, a : a + PAD_K])

    def to_core(h):
        rows = pl.ds(pl.multiple_of(h * PART + (1 - core) * HALF, 16), HALF)
        return remote(part_wire.at[rows], from_core.at[h], c_send.at[h], c_recv.at[h], sibling)

    for h in range(PARTS):
        for n, (a, b, s, row, lane) in enumerate(PAIRS):
            if (n in FIRST) == (h == 0) or (h == 0 and n == len(FIRST)):
                inner = acc[s, row : row + ROWS, lane : lane + PAD_K]
                part[n * ROWS : (n + 1) * ROWS] = sq_col[a] + sq_row[b] - 2.0 * inner
        rows = slice(h * PART, (h + 1) * PART)
        part_wire[rows] = part[rows].astype(bf16)
        to_core(h).start()
    start_g(2)

    def to_y(h, r):
        y2, device = y_peer(r)
        rows = pl.ds(pl.multiple_of(y2 * QUARTER, 16), QUARTER)
        return remote(core_wire.at[h, rows], from_y.at[h, r], y_send.at[h, r], y_recv.at[h, r], device)

    def to_plane(h, r):
        m2, device = plane_peer(r)
        rows = pl.ds(pl.multiple_of(m2 * CHUNK, 8), CHUNK)
        return remote(y_sum.at[h, rows], from_zx.at[h, r], p_send.at[h, r], p_recv.at[h, r], device)

    def mine(h):
        return pl.ds(pl.multiple_of(h * PART + core * HALF + y * QUARTER + member * CHUNK, 16), CHUNK)

    def kern_to_plane(h, r):
        rows = kern.at[mine(h)]
        return remote(rows, rows, ap_send.at[h, r], ap_recv.at[h, r], plane_peer(r)[1])

    def kern_to_y(h, r):
        rows = kern.at[pl.ds(pl.multiple_of(h * PART + core * HALF + y * QUARTER, 16), QUARTER)]
        return remote(rows, rows, ay_send.at[h, r], ay_recv.at[h, r], y_peer(r)[1])

    def kern_to_core(h, r):
        y2 = (y + 4 - r) % 4
        rows = kern.at[pl.ds(pl.multiple_of(h * PART + core * HALF + y2 * QUARTER, 16), QUARTER)]
        return remote(rows, rows, ac_send.at[h, r], ac_recv.at[h, r], sibling)

    for h in range(PARTS):
        to_core(h).wait_recv()
        rows = pl.ds(pl.multiple_of(h * PART + core * HALF, 16), HALF)
        core_sum[h] = part[rows] + from_core[h].astype(f32)
        core_wire[h] = core_sum[h].astype(bf16)
        for r in range(1, 4):
            to_y(h, r).start()
    for h in range(PARTS):
        for r in range(1, 4):
            to_y(h, r).wait_recv()
        total = core_sum[h, pl.ds(pl.multiple_of(y * QUARTER, 16), QUARTER)]
        for r in range(1, 4):
            total = total + from_y[h, r].astype(f32)
        y_sum[h] = total

        @pl.loop(1, 16)
        def _(r):
            to_plane(h, r).start()

    start_g(3)
    width = DIMS * spread[0]
    for h in range(PARTS):
        from_zx[h, 0] = y_sum[h, pl.ds(pl.multiple_of(member * CHUNK, 8), CHUNK)]

        @pl.loop(1, 16)
        def _(r):
            to_plane(h, r).wait_recv()

        kern[mine(h)] = jnp.exp(-jnp.sum(from_zx[h], axis=0) / width).astype(bf16)

        @pl.loop(1, 16)
        def _(r):
            kern_to_plane(h, r).start()

    start_g(4)

    for h in range(PARTS):
        @pl.loop(1, 16)
        def _(r):
            kern_to_plane(h, r).wait_recv()

        for r in range(1, 4):
            kern_to_y(h, r).start()
        kern_to_core(h, 0).start()
    start_g(5)
    for h in range(PARTS):
        for r in range(1, 4):
            kern_to_y(h, r).wait_recv()
            kern_to_core(h, r).start()

    real = lax.broadcasted_iota(jnp.int32, (PAD_K, PAD_K), 1) < ROWS
    for h in range(PARTS):
        for r in range(4):
            kern_to_core(h, r).wait_recv()
        rows = slice(h * PART, (h + 1) * PART)
        kern_wide[rows] = kern[rows].astype(f32)
        for n, (a, b, s, row, lane) in enumerate(PAIRS):
            if (n in FIRST) == (h == 0):
                block = kern_wide[n * ROWS : n * ROWS + PAD_K]
                square = jnp.where(real, block, 0.0)
                full[a * PAD_M : a * PAD_M + ROWS, b * PAD_K : (b + 1) * PAD_K] = square[:ROWS].astype(bf16)
                if a != b:
                    across = jnp.where(real, block.T, 0.0)
                    full[b * PAD_M : b * PAD_M + ROWS, a * PAD_K : (a + 1) * PAD_K] = across[:ROWS].astype(bf16)

    @pl.loop(0, BLOCKS)
    def _(i):
        rows = pl.ds(pl.multiple_of(i * PAD_M, 16), ROWS)
        sums = jnp.zeros((ROWS, PAD_K), f32)
        for k in range(BLOCKS):
            sums = sums + full[rows, k * PAD_K : (k + 1) * PAD_K].astype(f32)
        totals[i] = jnp.sum(sums, axis=1, keepdims=True)

    def outward(src, dst, send, recv, c, r):
        to = dom_peer(r)
        return remote(src.at[c, to], dst.at[c, dom], send.at[c, r], recv.at[c, r], (to, feat))

    def r_out(c, r):
        return outward(repel_stage, repel_land, r_send, r_recv, c, r)

    def d_out(c, r):
        return outward(drive_stage, drive_land, d_send, d_recv, c, r)

    def product_rows(i):
        return product[pl.ds(pl.multiple_of(i * PAD_M, 8), ROWS)]

    def repel_rows(c, i):
        here = xd[c, pl.ds(pl.multiple_of(i * PAD_K, 16), ROWS)].astype(f32)
        return totals[i] * here - product_rows(i)

    @pl.loop(0, PIECES)
    def _(c):
        product[...] = jnp.dot(full[...], xd[c], preferred_element_type=f32)

        @pl.loop(1, BLOCKS)
        def _(r):
            i = dom_peer(r)
            repel_stage[c, i] = repel_rows(c, i).astype(bf16)
            r_out(c, r).start()

        repel_out[:, columns(dom, c)] = repel_rows(c, dom)

    for c in range(PIECES):
        own_copy(g, gt, 1, c).wait()

        for p in (2 * c, 2 * c + 1):
            @pl.loop(1, BLOCKS)
            def _(r):
                g_in(p, r).wait()

        spread_out(gt, gd, c)

    @pl.loop(0, PIECES)
    def _(c):
        product[...] = jnp.dot(full[...], gd[c], preferred_element_type=f32)

        @pl.loop(1, BLOCKS)
        def _(r):
            i = dom_peer(r)
            drive_stage[c, i] = product_rows(i).astype(bf16)
            d_out(c, r).start()

        drive_out[:, columns(dom, c)] = product_rows(dom)

    for h in range(PARTS):
        to_core(h).wait_send()
        for r in range(1, 4):
            to_y(h, r).wait_send()
            kern_to_y(h, r).wait_send()
        for r in range(4):
            kern_to_core(h, r).wait_send()

        @pl.loop(1, 16)
        def _(r):
            to_plane(h, r).wait_send()
            kern_to_plane(h, r).wait_send()

    def widen(copy, land, out):
        @pl.loop(0, PIECES)
        def _(c):
            @pl.loop(1, BLOCKS)
            def _(r):
                copy(c, r).wait()
                source = (z + 4 - r // 2) % 4 * 2 + (x_lo + r % 2) % 2
                out[:, columns(source, c)] = land[c, source].astype(f32)

    widen(r_out, repel_land, repel_out)
    widen(d_out, drive_land, drive_out)


def per_device(particles, gradients, spread):
    bf16, f32 = jnp.bfloat16, jnp.float32
    vmem, dma = pltpu.VMEM, pltpu.SemaphoreType.DMA
    slab, dense = (PIECES, BLOCKS, ROWS, PIECE), (PIECES, BLOCKS * PAD_K, PIECE)
    drive, repel = pl.pallas_call(
        kernel,
        out_shape=[pltpu.VMEM((ROWS, COLS), f32)] * 2,
        in_specs=[pl.BlockSpec(memory_space=pl.ANY)] * 2 + [pl.BlockSpec(memory_space=pltpu.SMEM)],
        out_specs=[pl.BlockSpec(memory_space=pltpu.VMEM)] * 2,
        scratch_shapes=[
            vmem(slab, bf16), vmem(slab, bf16), vmem(dense, bf16), vmem(dense, bf16),
            vmem((len(SUPER), 2 * PAD_K, 2 * PAD_K), f32), vmem((FLAT, 128), f32), vmem((FLAT, 128), bf16),
            vmem((PARTS, HALF, 128), bf16), vmem((PARTS, HALF, 128), f32), vmem((PARTS, HALF, 128), bf16),
            vmem((PARTS, 4, QUARTER, 128), bf16), vmem((PARTS, QUARTER, 128), f32), vmem((PARTS, 16, CHUNK, 128), f32),
            vmem((FLAT, 128), bf16), vmem((FLAT, 128), f32), vmem((BLOCKS * PAD_M, BLOCKS * PAD_K), bf16),
            vmem((BLOCKS, ROWS, 1), f32), vmem((BLOCKS * PAD_M, PIECE), f32),
            vmem(slab, bf16), vmem(slab, bf16), vmem(slab, bf16), vmem(slab, bf16),
        ]
        + [dma((PIECES, BLOCKS))] * 2 + [dma((G_PIECES, BLOCKS))] * 2 + [dma((PIECES, BLOCKS))] * 4 + [dma((2, PIECES))]
        + [dma((PARTS,))] * 2 + [dma((PARTS, 4))] * 2
        + [dma((PARTS, 16))] * 4 + [dma((PARTS, 4))] * 4,
        compiler_params=pltpu.CompilerParams(
            collective_id=0, has_side_effects=True, vmem_limit_bytes=44 * 2**20),
        name="svgd",
    )(particles, gradients, spread)
    return drive, repel


def solution(mesh):
    return jax.shard_map(
        per_device,
        mesh=mesh,
        in_specs=(P("dom", "feat"), P("dom", "feat"), P()),
        out_specs=(P("dom", "feat"), P("dom", "feat")),
        check_vma=False,
    )
```

```python
import jax
import jax.numpy as jnp
from jax import lax
from jax.experimental import pallas as pl
from jax.experimental.pallas import tpu as pltpu
from jax.sharding import PartitionSpec as P

DIMS = 196608
ROWS = 104
PAD_K, PAD_M = 128, 112
COLS = 12288
BLOCKS = 8
PIECES = 3
WIDTH = COLS // BLOCKS
PIECE = WIDTH // PIECES
G_PIECES = 12
G_PIECE = WIDTH // G_PIECES
G_RATIO = G_PIECES // PIECES
G_AT = (2, 2, 1, 0, 1, 1, 5)
PARTS = 2
FLAT = 4096
PART = FLAT // PARTS
HALF, QUARTER, CHUNK = PART // 2, PART // 8, PART // 128
SUPER = [(i, i) for i in range(4)] + [(i, j) for i in range(4) for j in range(i + 1, 4)]
PAIRS = []
for n, (si, sj) in enumerate(SUPER):
    for a in range(2):
        for b in range(2):
            if 2 * si + a <= 2 * sj + b:
                PAIRS.append((2 * si + a, 2 * sj + b, n, a * PAD_K, b * PAD_K))
FIRST = [n for n in range(len(PAIRS)) if (n + 1) * ROWS <= PART]
HOPS = (0, 1, 2, 1)
PLANE = sorted(range(1, 16), key=lambda r: -HOPS[r // 4] - HOPS[r % 4])
RING = (2, 1, 3)
MESH = pl.DeviceIdType.MESH


def kernel(
    x, g, spread, drive_out, repel_out,
    xt, gt, xd, gd, acc, part, part_wire, from_core, core_sum, core_wire, from_y, y_sum, from_zx,
    kern, kern_wide, full, totals, product, drive_stage, repel_stage, drive_land, repel_land,
    x_send, x_recv, g_send, g_recv, d_send, d_recv, r_send, r_recv, own_sem,
    c_send, c_recv, y_send, y_recv, p_send, p_recv, ap_send, ap_recv, ay_send, ay_recv, ac_send, ac_recv,
):
    f32, bf16 = jnp.float32, jnp.bfloat16
    dom, feat = lax.axis_index("dom"), lax.axis_index("feat")
    z, x_lo = dom // 2, dom % 2
    y, x_hi, core = feat // 4, (feat // 2) % 2, feat % 2
    xx = x_hi * 2 + x_lo
    member = z * 4 + xx

    def dom_peer(r):
        return (z + r // 2) % 4 * 2 + (x_lo + r % 2) % 2

    def plane_peer(r):
        z2, x2 = (z + r // 4) % 4, (xx + r % 4) % 4
        return z2 * 4 + x2, (z2 * 2 + x2 % 2, y * 4 + x2 // 2 * 2 + core)

    def y_peer(r):
        y2 = (y + r) % 4
        return y2, (dom, y2 * 4 + x_hi * 2 + core)

    sibling = (dom, y * 4 + x_hi * 2 + 1 - core)

    barrier = pltpu.get_barrier_semaphore()

    @pl.loop(1, 16)
    def _(r):
        pl.semaphore_signal(barrier, inc=1, device_id=plane_peer(r)[1], device_id_type=MESH)

    @pl.loop(1, 4)
    def _(r):
        pl.semaphore_signal(barrier, inc=1, device_id=y_peer(r)[1], device_id_type=MESH)

    pl.semaphore_signal(barrier, inc=1, device_id=sibling, device_id_type=MESH)
    pl.semaphore_wait(barrier, 19)

    def columns(block, c):
        return pl.ds(pl.multiple_of(block * WIDTH + c * PIECE, 128), PIECE)

    def remote(src, dst, send, recv, device):
        return pltpu.make_async_remote_copy(
            src_ref=src, dst_ref=dst, send_sem=send, recv_sem=recv, device_id=device, device_id_type=MESH)

    def all_of(ref, sem):
        pltpu.make_async_copy(ref, ref, sem).wait()

    def inward(src, dst, send, recv, c, r):
        to = dom_peer(r)
        return remote(src.at[:, columns(to, c)], dst.at[c, dom], send.at[c, r], recv.at[c, r], (to, feat))

    def x_in(c, r):
        return inward(x, xt, x_send, x_recv, c, r)

    def g_in(p, r):
        to, lane = dom_peer(r), p % G_RATIO * G_PIECE
        source = g.at[:, pl.ds(pl.multiple_of(to * WIDTH + p * G_PIECE, 128), G_PIECE)]
        target = gt.at[p // G_RATIO, dom, :, pl.ds(lane, G_PIECE)]
        return remote(source, target, g_send.at[p, r], g_recv.at[p, r], (to, feat))

    def start_g(point):
        for p in range(sum(G_AT[:point]), sum(G_AT[: point + 1])):
            @pl.loop(1, BLOCKS)
            def _(r):
                g_in(p, r).start()

    def own_copy(src, dst, which, c):
        return pltpu.make_async_copy(src.at[:, columns(dom, c)], dst.at[c, dom], own_sem.at[which, c])

    for c in range(2):
        @pl.loop(1, BLOCKS)
        def _(r):
            x_in(c, r).start()

    for c in range(PIECES):
        own_copy(x, xt, 0, c).start()
    for c in range(PIECES):
        own_copy(g, gt, 1, c).start()
    part[FLAT - 3 * PAD_K :] = jnp.zeros((3 * PAD_K, 128), f32)

    def spread_out(src, dst, c):
        @pl.loop(0, BLOCKS)
        def _(b):
            start = pl.multiple_of(b * PAD_K, PAD_K)
            dst[c, pl.ds(start + PAD_K - 32, 32)] = jnp.zeros((32, PIECE), bf16)
            dst[c, pl.ds(start, ROWS)] = src[c, b]

    for c in range(PIECES):
        @pl.loop(1, BLOCKS)
        def _(r):
            x_in(c, r).wait_send()
            if c == 0:
                x_in(2, r).start()

        if c > 0:
            start_g(c - 1)
        own_copy(x, xt, 0, c).wait()

        @pl.loop(1, BLOCKS)
        def _(r):
            x_in(c, r).wait_recv()

        spread_out(xt, xd, c)
        for n, (si, sj) in enumerate(SUPER):
            left = xd[c, si * 2 * PAD_K : (si + 1) * 2 * PAD_K]
            right = xd[c, sj * 2 * PAD_K : (sj + 1) * 2 * PAD_K]
            inner = lax.dot_general(left, right, (((1,), (1,)), ((), ())), preferred_element_type=f32)
            acc[n] = inner if c == 0 else acc[n] + inner

    size = (2 * PAD_K, 2 * PAD_K)
    on_diagonal = lax.broadcasted_iota(jnp.int32, size, 0) == lax.broadcasted_iota(jnp.int32, size, 1)
    sq_col, sq_row = [], []
    for n in range(4):
        picked = jnp.where(on_diagonal, acc[n], 0.0)
        col, row = jnp.sum(picked, axis=1, keepdims=True), jnp.sum(picked, axis=0, keepdims=True)
        for a in (0, PAD_K):
            sq_col.append(col[a : a + ROWS])
            sq_row.append(row[:, a : a + PAD_K])

    def to_core(h):
        rows = pl.ds(pl.multiple_of(h * PART + (1 - core) * HALF, 16), HALF)
        return remote(part_wire.at[rows], from_core.at[h], c_send.at[h], c_recv.at[h], sibling)

    for h in range(PARTS):
        for n, (a, b, s, row, lane) in enumerate(PAIRS):
            if (n in FIRST) == (h == 0) or (h == 0 and n == len(FIRST)):
                inner = acc[s, row : row + ROWS, lane : lane + PAD_K]
                part[n * ROWS : (n + 1) * ROWS] = sq_col[a] + sq_row[b] - 2.0 * inner
        rows = slice(h * PART, (h + 1) * PART)
        part_wire[rows] = part[rows].astype(bf16)
        to_core(h).start()
    start_g(2)

    def to_y(h, r):
        y2, device = y_peer(r)
        rows = pl.ds(pl.multiple_of(y2 * QUARTER, 16), QUARTER)
        return remote(core_wire.at[h, rows], from_y.at[h, r], y_send.at[h, r], y_recv.at[h, r], device)

    def to_plane(h, r):
        m2, device = plane_peer(r)
        rows = pl.ds(pl.multiple_of(m2 * CHUNK, 8), CHUNK)
        return remote(y_sum.at[h, rows], from_zx.at[h, r], p_send.at[h], p_recv.at[h], device)

    def mine(h):
        return pl.ds(pl.multiple_of(h * PART + core * HALF + y * QUARTER + member * CHUNK, 16), CHUNK)

    def kern_to_plane(h, r):
        rows = kern.at[mine(h)]
        return remote(rows, rows, ap_send.at[h], ap_recv.at[h], plane_peer(r)[1])

    def kern_to_y(h, r):
        rows = kern.at[pl.ds(pl.multiple_of(h * PART + core * HALF + y * QUARTER, 16), QUARTER)]
        return remote(rows, rows, ay_send.at[h, r], ay_recv.at[h, r], y_peer(r)[1])

    def kern_to_core(h, r):
        y2 = (y + 4 - r) % 4
        rows = kern.at[pl.ds(pl.multiple_of(h * PART + core * HALF + y2 * QUARTER, 16), QUARTER)]
        return remote(rows, rows, ac_send.at[h, r], ac_recv.at[h, r], sibling)

    for h in range(PARTS):
        to_core(h).wait_recv()
        rows = pl.ds(pl.multiple_of(h * PART + core * HALF, 16), HALF)
        core_sum[h] = part[rows] + from_core[h].astype(f32)
        core_wire[h] = core_sum[h].astype(bf16)
        for r in RING:
            to_y(h, r).start()
    for h in range(PARTS):
        for r in range(1, 4):
            to_y(h, r).wait_recv()
        total = core_sum[h, pl.ds(pl.multiple_of(y * QUARTER, 16), QUARTER)]
        for r in range(1, 4):
            total = total + from_y[h, r].astype(f32)
        y_sum[h] = total

        for r in PLANE:
            to_plane(h, r).start()

        start_g(3 + h)

    width = DIMS * spread[0]
    for h in range(PARTS):
        from_zx[h, 0] = y_sum[h, pl.ds(pl.multiple_of(member * CHUNK, 8), CHUNK)]

        all_of(from_zx.at[h, pl.ds(1, 15)], p_recv.at[h])

        kern[mine(h)] = jnp.exp(-jnp.sum(from_zx[h], axis=0) / width).astype(bf16)

        for r in PLANE:
            kern_to_plane(h, r).start()

        start_g(5 + h)

    for h in range(PARTS):
        all_of(kern.at[pl.ds(0, 15 * CHUNK)], ap_recv.at[h])

        for r in RING:
            kern_to_y(h, r).start()
        kern_to_core(h, 0).start()
    for h in range(PARTS):
        for r in range(1, 4):
            kern_to_y(h, r).wait_recv()
            kern_to_core(h, r).start()

    real = lax.broadcasted_iota(jnp.int32, (PAD_K, PAD_K), 1) < ROWS
    for h in range(PARTS):
        for r in range(4):
            kern_to_core(h, r).wait_recv()
        rows = slice(h * PART, (h + 1) * PART)
        kern_wide[rows] = kern[rows].astype(f32)
        for n, (a, b, s, row, lane) in enumerate(PAIRS):
            if (n in FIRST) == (h == 0):
                block = kern_wide[n * ROWS : n * ROWS + PAD_K]
                square = jnp.where(real, block, 0.0)
                full[a * PAD_M : a * PAD_M + ROWS, b * PAD_K : (b + 1) * PAD_K] = square[:ROWS].astype(bf16)
                if a != b:
                    across = jnp.where(real, block.T, 0.0)
                    full[b * PAD_M : b * PAD_M + ROWS, a * PAD_K : (a + 1) * PAD_K] = across[:ROWS].astype(bf16)

    ones = jnp.ones((BLOCKS * PAD_K, PAD_K), bf16)
    totals[...] = jnp.dot(full[...], ones, preferred_element_type=f32)

    def outward(src, dst, send, recv, c, r):
        to = dom_peer(r)
        return remote(src.at[c, to], dst.at[c, dom], send.at[c, r], recv.at[c, r], (to, feat))

    def r_out(c, r):
        return outward(repel_stage, repel_land, r_send, r_recv, c, r)

    def d_out(c, r):
        return outward(drive_stage, drive_land, d_send, d_recv, c, r)

    def product_rows(i):
        return product[pl.ds(pl.multiple_of(i * PAD_M, 8), ROWS)]

    def repel_rows(c, i):
        here = xd[c, pl.ds(pl.multiple_of(i * PAD_K, 16), ROWS)].astype(f32)
        total = totals[pl.ds(pl.multiple_of(i * PAD_M, 8), ROWS)]
        return jnp.concatenate([total] * (PIECE // PAD_K), axis=1) * here - product_rows(i)

    @pl.loop(0, PIECES)
    def _(c):
        product[...] = jnp.dot(full[...], xd[c], preferred_element_type=f32)

        @pl.loop(1, BLOCKS)
        def _(r):
            i = dom_peer(r)
            repel_stage[c, i] = repel_rows(c, i).astype(bf16)
            r_out(c, r).start()

        repel_out[:, columns(dom, c)] = repel_rows(c, dom)

    for c in range(PIECES):
        own_copy(g, gt, 1, c).wait()

        for p in range(G_RATIO * c, G_RATIO * (c + 1)):
            @pl.loop(1, BLOCKS)
            def _(r):
                g_in(p, r).wait()

        spread_out(gt, gd, c)

    @pl.loop(0, PIECES)
    def _(c):
        product[...] = jnp.dot(full[...], gd[c], preferred_element_type=f32)

        @pl.loop(1, BLOCKS)
        def _(r):
            i = dom_peer(r)
            drive_stage[c, i] = product_rows(i).astype(bf16)
            d_out(c, r).start()

        drive_out[:, columns(dom, c)] = product_rows(dom)

    for h in range(PARTS):
        to_core(h).wait_send()
        for r in range(1, 4):
            to_y(h, r).wait_send()
            kern_to_y(h, r).wait_send()
        for r in range(4):
            kern_to_core(h, r).wait_send()

        all_of(from_zx.at[h, pl.ds(1, 15)], p_send.at[h])
        all_of(kern.at[pl.ds(0, 15 * CHUNK)], ap_send.at[h])

    def widen(copy, land, out):
        @pl.loop(0, PIECES)
        def _(c):
            @pl.loop(1, BLOCKS)
            def _(r):
                copy(c, r).wait()
                source = (z + 4 - r // 2) % 4 * 2 + (x_lo + r % 2) % 2
                out[:, columns(source, c)] = land[c, source].astype(f32)

    widen(r_out, repel_land, repel_out)
    widen(d_out, drive_land, drive_out)


def per_device(particles, gradients, spread):
    bf16, f32 = jnp.bfloat16, jnp.float32
    vmem, dma = pltpu.VMEM, pltpu.SemaphoreType.DMA
    slab, dense = (PIECES, BLOCKS, ROWS, PIECE), (PIECES, BLOCKS * PAD_K, PIECE)
    drive, repel = pl.pallas_call(
        kernel,
        out_shape=[pltpu.VMEM((ROWS, COLS), f32)] * 2,
        in_specs=[pl.BlockSpec(memory_space=pl.ANY)] * 2 + [pl.BlockSpec(memory_space=pltpu.SMEM)],
        out_specs=[pl.BlockSpec(memory_space=pltpu.VMEM)] * 2,
        scratch_shapes=[
            vmem(slab, bf16), vmem(slab, bf16), vmem(dense, bf16), vmem(dense, bf16),
            vmem((len(SUPER), 2 * PAD_K, 2 * PAD_K), f32), vmem((FLAT, 128), f32), vmem((FLAT, 128), bf16),
            vmem((PARTS, HALF, 128), bf16), vmem((PARTS, HALF, 128), f32), vmem((PARTS, HALF, 128), bf16),
            vmem((PARTS, 4, QUARTER, 128), bf16), vmem((PARTS, QUARTER, 128), f32), vmem((PARTS, 16, CHUNK, 128), f32),
            vmem((FLAT, 128), bf16), vmem((FLAT, 128), f32), vmem((BLOCKS * PAD_M, BLOCKS * PAD_K), bf16),
            vmem((BLOCKS * PAD_M, PAD_K), f32), vmem((BLOCKS * PAD_M, PIECE), f32),
            vmem(slab, bf16), vmem(slab, bf16), vmem(slab, bf16), vmem(slab, bf16),
        ]
        + [dma((PIECES, BLOCKS))] * 2 + [dma((G_PIECES, BLOCKS))] * 2 + [dma((PIECES, BLOCKS))] * 4 + [dma((2, PIECES))]
        + [dma((PARTS,))] * 2 + [dma((PARTS, 4))] * 2
        + [dma((PARTS,))] * 4 + [dma((PARTS, 4))] * 4,
        compiler_params=pltpu.CompilerParams(
            collective_id=0, has_side_effects=True, vmem_limit_bytes=44 * 2**20),
        name="svgd",
    )(particles, gradients, spread)
    return drive, repel


def solution(mesh):
    return jax.shard_map(
        per_device,
        mesh=mesh,
        in_specs=(P("dom", "feat"), P("dom", "feat"), P()),
        out_specs=(P("dom", "feat"), P("dom", "feat")),
        check_vma=False,
    )
```

```python
import jax
import jax.numpy as jnp
from jax import lax
from jax.experimental import pallas as pl
from jax.experimental.pallas import tpu as pltpu
from jax.sharding import PartitionSpec as P

DIMS = 196608
ROWS = 104
PAD_K, PAD_M = 128, 112
COLS = 12288
BLOCKS = 8
PIECES = 3
WIDTH = COLS // BLOCKS
PIECE = WIDTH // PIECES
G_WIDTHS = (256, 256, 128, 128, 128, 128, 512)
G_STARTS = tuple(sum(G_WIDTHS[:p]) for p in range(len(G_WIDTHS)))
G_AT = (1, 1, 1, 0, 1, 1, 2)
PARTS = 2
FLAT = 4096
PART = FLAT // PARTS
HALF, QUARTER, CHUNK = PART // 2, PART // 8, PART // 128
SUPER = [(i, i) for i in range(4)] + [(i, j) for i in range(4) for j in range(i + 1, 4)]
PAIRS = []
for n, (si, sj) in enumerate(SUPER):
    for a in range(2):
        for b in range(2):
            if 2 * si + a <= 2 * sj + b:
                PAIRS.append((2 * si + a, 2 * sj + b, n, a * PAD_K, b * PAD_K))
FIRST = [n for n in range(len(PAIRS)) if (n + 1) * ROWS <= PART]
HOPS = (0, 1, 2, 1)
PLANE = sorted(range(1, 16), key=lambda r: -HOPS[r // 4] - HOPS[r % 4])
RING = (2, 1, 3)
MESH = pl.DeviceIdType.MESH


def kernel(
    x, g, spread, drive_out, repel_out,
    xt, gt, xd, gd, acc, part, part_wire, from_core, core_sum, core_wire, from_y, y_sum, from_zx,
    kern, kern_wide, full, totals, product, drive_stage, repel_stage, drive_land, repel_land,
    x_send, x_recv, g_send, g_recv, d_send, d_recv, r_send, r_recv, own_sem,
    c_send, c_recv, y_send, y_recv, p_send, p_recv, ap_send, ap_recv, ay_send, ay_recv, ac_send, ac_recv,
):
    f32, bf16 = jnp.float32, jnp.bfloat16
    dom, feat = lax.axis_index("dom"), lax.axis_index("feat")
    z, x_lo = dom // 2, dom % 2
    y, x_hi, core = feat // 4, (feat // 2) % 2, feat % 2
    xx = x_hi * 2 + x_lo
    member = z * 4 + xx

    def dom_peer(r):
        return (z + r // 2) % 4 * 2 + (x_lo + r % 2) % 2

    def plane_peer(r):
        z2, x2 = (z + r // 4) % 4, (xx + r % 4) % 4
        return z2 * 4 + x2, (z2 * 2 + x2 % 2, y * 4 + x2 // 2 * 2 + core)

    def y_peer(r):
        y2 = (y + r) % 4
        return y2, (dom, y2 * 4 + x_hi * 2 + core)

    sibling = (dom, y * 4 + x_hi * 2 + 1 - core)

    barrier = pltpu.get_barrier_semaphore()

    @pl.loop(1, 16)
    def _(r):
        pl.semaphore_signal(barrier, inc=1, device_id=plane_peer(r)[1], device_id_type=MESH)

    @pl.loop(1, 4)
    def _(r):
        pl.semaphore_signal(barrier, inc=1, device_id=y_peer(r)[1], device_id_type=MESH)

    pl.semaphore_signal(barrier, inc=1, device_id=sibling, device_id_type=MESH)
    pl.semaphore_wait(barrier, 19)

    def columns(block, c):
        return pl.ds(pl.multiple_of(block * WIDTH + c * PIECE, 128), PIECE)

    def remote(src, dst, send, recv, device):
        return pltpu.make_async_remote_copy(
            src_ref=src, dst_ref=dst, send_sem=send, recv_sem=recv, device_id=device, device_id_type=MESH)

    def all_of(ref, sem):
        pltpu.make_async_copy(ref, ref, sem).wait()

    def inward(src, dst, send, recv, start, width, r):
        to, c = dom_peer(r), start // PIECE
        source = src.at[:, pl.ds(pl.multiple_of(to * WIDTH + start, 128), width)]
        target = dst.at[c, dom, :, pl.ds(start % PIECE, width)]
        return remote(source, target, send.at[c], recv.at[c], (to, feat))

    def to_all(start_one):
        @pl.loop(0, BLOCKS - 1)
        def _(q):
            start_one(BLOCKS - 1 - q)

    def all_seven(slab, sem, c):
        all_of(slab.at[c, pl.ds(0, BLOCKS - 1)], sem.at[c])

    def start_x(c):
        to_all(lambda r: inward(x, xt, x_send, x_recv, c * PIECE, PIECE, r).start())

    def start_g(point):
        for p in range(sum(G_AT[:point]), sum(G_AT[: point + 1])):
            to_all(lambda r: inward(g, gt, g_send, g_recv, G_STARTS[p], G_WIDTHS[p], r).start())

    def own_copy(src, dst, which, c):
        return pltpu.make_async_copy(src.at[:, columns(dom, c)], dst.at[c, dom], own_sem.at[which, c])

    for c in range(PIECES):
        start_x(c)
    for c in range(PIECES):
        own_copy(x, xt, 0, c).start()
    for c in range(PIECES):
        own_copy(g, gt, 1, c).start()
    part[FLAT - 3 * PAD_K :] = jnp.zeros((3 * PAD_K, 128), f32)

    def spread_out(src, dst, c):
        @pl.loop(0, BLOCKS)
        def _(b):
            start = pl.multiple_of(b * PAD_K, PAD_K)
            dst[c, pl.ds(start + PAD_K - 32, 32)] = jnp.zeros((32, PIECE), bf16)
            dst[c, pl.ds(start, ROWS)] = src[c, b]

    for c in range(PIECES):
        all_seven(xt, x_send, c)
        if c > 0:
            start_g(c - 1)
        own_copy(x, xt, 0, c).wait()
        all_seven(xt, x_recv, c)
        spread_out(xt, xd, c)
        for n, (si, sj) in enumerate(SUPER):
            left = xd[c, si * 2 * PAD_K : (si + 1) * 2 * PAD_K]
            right = xd[c, sj * 2 * PAD_K : (sj + 1) * 2 * PAD_K]
            inner = lax.dot_general(left, right, (((1,), (1,)), ((), ())), preferred_element_type=f32)
            acc[n] = inner if c == 0 else acc[n] + inner

    size = (2 * PAD_K, 2 * PAD_K)
    on_diagonal = lax.broadcasted_iota(jnp.int32, size, 0) == lax.broadcasted_iota(jnp.int32, size, 1)
    sq_col, sq_row = [], []
    for n in range(4):
        picked = jnp.where(on_diagonal, acc[n], 0.0)
        col, row = jnp.sum(picked, axis=1, keepdims=True), jnp.sum(picked, axis=0, keepdims=True)
        for a in (0, PAD_K):
            sq_col.append(col[a : a + ROWS])
            sq_row.append(row[:, a : a + PAD_K])

    def to_core(h):
        rows = pl.ds(pl.multiple_of(h * PART + (1 - core) * HALF, 16), HALF)
        return remote(part_wire.at[rows], from_core.at[h], c_send.at[h], c_recv.at[h], sibling)

    for h in range(PARTS):
        for n, (a, b, s, row, lane) in enumerate(PAIRS):
            if (n in FIRST) == (h == 0) or (h == 0 and n == len(FIRST)):
                inner = acc[s, row : row + ROWS, lane : lane + PAD_K]
                part[n * ROWS : (n + 1) * ROWS] = sq_col[a] + sq_row[b] - 2.0 * inner
        rows = slice(h * PART, (h + 1) * PART)
        part_wire[rows] = part[rows].astype(bf16)
        to_core(h).start()
    start_g(2)

    def to_y(h, r):
        y2, device = y_peer(r)
        rows = pl.ds(pl.multiple_of(y2 * QUARTER, 16), QUARTER)
        return remote(core_wire.at[h, rows], from_y.at[h, r], y_send.at[h], y_recv.at[h], device)

    def to_plane(h, r):
        m2, device = plane_peer(r)
        rows = pl.ds(pl.multiple_of(m2 * CHUNK, 8), CHUNK)
        return remote(y_sum.at[h, rows], from_zx.at[h, r], p_send.at[h], p_recv.at[h], device)

    def mine(h):
        return pl.ds(pl.multiple_of(h * PART + core * HALF + y * QUARTER + member * CHUNK, 16), CHUNK)

    def kern_to_plane(h, r):
        rows = kern.at[mine(h)]
        return remote(rows, rows, ap_send.at[h], ap_recv.at[h], plane_peer(r)[1])

    def kern_to_y(h, r):
        rows = kern.at[pl.ds(pl.multiple_of(h * PART + core * HALF + y * QUARTER, 16), QUARTER)]
        return remote(rows, rows, ay_send.at[h, r], ay_recv.at[h, r], y_peer(r)[1])

    def kern_to_core(h, r):
        y2 = (y + 4 - r) % 4
        rows = kern.at[pl.ds(pl.multiple_of(h * PART + core * HALF + y2 * QUARTER, 16), QUARTER)]
        return remote(rows, rows, ac_send.at[h, r], ac_recv.at[h, r], sibling)

    for h in range(PARTS):
        to_core(h).wait_recv()
        rows = pl.ds(pl.multiple_of(h * PART + core * HALF, 16), HALF)
        core_sum[h] = part[rows] + from_core[h].astype(f32)
        core_wire[h] = core_sum[h].astype(bf16)
        for r in RING:
            to_y(h, r).start()
    for h in range(PARTS):
        all_of(from_y.at[h, pl.ds(1, 3)], y_recv.at[h])
        total = core_sum[h, pl.ds(pl.multiple_of(y * QUARTER, 16), QUARTER)]
        for r in range(1, 4):
            total = total + from_y[h, r].astype(f32)
        y_sum[h] = total

        for r in PLANE:
            to_plane(h, r).start()

        start_g(3 + h)

    width = DIMS * spread[0]
    for h in range(PARTS):
        from_zx[h, 0] = y_sum[h, pl.ds(pl.multiple_of(member * CHUNK, 8), CHUNK)]

        all_of(from_zx.at[h, pl.ds(1, 15)], p_recv.at[h])

        kern[mine(h)] = jnp.exp(-jnp.sum(from_zx[h], axis=0) / width).astype(bf16)

        for r in PLANE:
            kern_to_plane(h, r).start()

        start_g(5 + h)

    for h in range(PARTS):
        all_of(kern.at[pl.ds(0, 15 * CHUNK)], ap_recv.at[h])

        for r in RING:
            kern_to_y(h, r).start()
        kern_to_core(h, 0).start()
    for h in range(PARTS):
        for r in range(1, 4):
            kern_to_y(h, r).wait_recv()
            kern_to_core(h, r).start()

    real = lax.broadcasted_iota(jnp.int32, (PAD_K, PAD_K), 1) < ROWS
    for h in range(PARTS):
        for r in range(4):
            kern_to_core(h, r).wait_recv()
        rows = slice(h * PART, (h + 1) * PART)
        kern_wide[rows] = kern[rows].astype(f32)
        for n, (a, b, s, row, lane) in enumerate(PAIRS):
            if (n in FIRST) == (h == 0):
                block = kern_wide[n * ROWS : n * ROWS + PAD_K]
                square = jnp.where(real, block, 0.0)
                full[a * PAD_M : a * PAD_M + ROWS, b * PAD_K : (b + 1) * PAD_K] = square[:ROWS].astype(bf16)
                if a != b:
                    across = jnp.where(real, block.T, 0.0)
                    full[b * PAD_M : b * PAD_M + ROWS, a * PAD_K : (a + 1) * PAD_K] = across[:ROWS].astype(bf16)

    ones = jnp.ones((BLOCKS * PAD_K, PAD_K), bf16)
    totals[...] = jnp.dot(full[...], ones, preferred_element_type=f32)

    def outward(src, dst, send, recv, c, r):
        to = dom_peer(r)
        return remote(src.at[c, to], dst.at[c, dom], send.at[c], recv.at[c], (to, feat))

    def r_out(c, r):
        return outward(repel_stage, repel_land, r_send, r_recv, c, r)

    def d_out(c, r):
        return outward(drive_stage, drive_land, d_send, d_recv, c, r)

    def product_rows(i):
        return product[pl.ds(pl.multiple_of(i * PAD_M, 8), ROWS)]

    def repel_rows(c, i):
        here = xd[c, pl.ds(pl.multiple_of(i * PAD_K, 16), ROWS)].astype(f32)
        total = totals[pl.ds(pl.multiple_of(i * PAD_M, 8), ROWS)]
        return jnp.concatenate([total] * (PIECE // PAD_K), axis=1) * here - product_rows(i)

    @pl.loop(0, PIECES)
    def _(c):
        product[...] = jnp.dot(full[...], xd[c], preferred_element_type=f32)

        def one(r):
            i = dom_peer(r)
            repel_stage[c, i] = repel_rows(c, i).astype(bf16)
            r_out(c, r).start()

        to_all(one)

        repel_out[:, columns(dom, c)] = repel_rows(c, dom)

    for c in range(PIECES):
        own_copy(g, gt, 1, c).wait()

        all_seven(gt, g_recv, c)
        spread_out(gt, gd, c)

    @pl.loop(0, PIECES)
    def _(c):
        product[...] = jnp.dot(full[...], gd[c], preferred_element_type=f32)

        def one(r):
            i = dom_peer(r)
            drive_stage[c, i] = product_rows(i).astype(bf16)
            d_out(c, r).start()

        to_all(one)

        drive_out[:, columns(dom, c)] = product_rows(dom)

    for h in range(PARTS):
        to_core(h).wait_send()
        all_of(from_y.at[h, pl.ds(1, 3)], y_send.at[h])
        for r in range(1, 4):
            kern_to_y(h, r).wait_send()
        for r in range(4):
            kern_to_core(h, r).wait_send()

        all_of(from_zx.at[h, pl.ds(1, 15)], p_send.at[h])
        all_of(kern.at[pl.ds(0, 15 * CHUNK)], ap_send.at[h])

    for c in range(PIECES):
        all_seven(gt, g_send, c)

    def widen(land, out, send, recv):
        @pl.loop(0, PIECES)
        def _(c):
            all_seven(land, send, c)
            all_seven(land, recv, c)

            @pl.loop(1, BLOCKS)
            def _(k):
                source = (dom + k) % BLOCKS
                out[:, columns(source, c)] = land[c, source].astype(f32)

    widen(repel_land, repel_out, r_send, r_recv)
    widen(drive_land, drive_out, d_send, d_recv)


def per_device(particles, gradients, spread):
    bf16, f32 = jnp.bfloat16, jnp.float32
    vmem, dma = pltpu.VMEM, pltpu.SemaphoreType.DMA
    slab, dense = (PIECES, BLOCKS, ROWS, PIECE), (PIECES, BLOCKS * PAD_K, PIECE)
    drive, repel = pl.pallas_call(
        kernel,
        out_shape=[pltpu.VMEM((ROWS, COLS), f32)] * 2,
        in_specs=[pl.BlockSpec(memory_space=pl.ANY)] * 2 + [pl.BlockSpec(memory_space=pltpu.SMEM)],
        out_specs=[pl.BlockSpec(memory_space=pltpu.VMEM)] * 2,
        scratch_shapes=[
            vmem(slab, bf16), vmem(slab, bf16), vmem(dense, bf16), vmem(dense, bf16),
            vmem((len(SUPER), 2 * PAD_K, 2 * PAD_K), f32), vmem((FLAT, 128), f32), vmem((FLAT, 128), bf16),
            vmem((PARTS, HALF, 128), bf16), vmem((PARTS, HALF, 128), f32), vmem((PARTS, HALF, 128), bf16),
            vmem((PARTS, 4, QUARTER, 128), bf16), vmem((PARTS, QUARTER, 128), f32), vmem((PARTS, 16, CHUNK, 128), f32),
            vmem((FLAT, 128), bf16), vmem((FLAT, 128), f32), vmem((BLOCKS * PAD_M, BLOCKS * PAD_K), bf16),
            vmem((BLOCKS * PAD_M, PAD_K), f32), vmem((BLOCKS * PAD_M, PIECE), f32),
            vmem(slab, bf16), vmem(slab, bf16), vmem(slab, bf16), vmem(slab, bf16),
        ]
        + [dma((PIECES,))] * 8 + [dma((2, PIECES))]
        + [dma((PARTS,))] * 4
        + [dma((PARTS,))] * 4 + [dma((PARTS, 4))] * 4,
        compiler_params=pltpu.CompilerParams(
            collective_id=0, has_side_effects=True, vmem_limit_bytes=44 * 2**20),
        name="svgd",
    )(particles, gradients, spread)
    return drive, repel


def solution(mesh):
    return jax.shard_map(
        per_device,
        mesh=mesh,
        in_specs=(P("dom", "feat"), P("dom", "feat"), P()),
        out_specs=(P("dom", "feat"), P("dom", "feat")),
        check_vma=False,
    )
```

```python
import jax
import jax.numpy as jnp
from jax import lax
from jax.experimental import pallas as pl
from jax.experimental.pallas import tpu as pltpu
from jax.sharding import PartitionSpec as P

DIMS = 196608
ROWS = 104
PAD_K, PAD_M = 128, 112
COLS = 12288
BLOCKS = 8
PIECES = 2
WIDTH = COLS // BLOCKS
PIECE = WIDTH // PIECES
G_WIDTHS = (256, 256, 128, 128, 128, 128, 512)
G_STARTS = tuple(sum(G_WIDTHS[:p]) for p in range(len(G_WIDTHS)))
G_AT = (2, 0, 1, 0, 1, 1, 2)
PARTS = 2
FLAT = 4096
PART = FLAT // PARTS
HALF, QUARTER, CHUNK = PART // 2, PART // 8, PART // 128
SUPER = [(i, i) for i in range(4)] + [(i, j) for i in range(4) for j in range(i + 1, 4)]
PAIRS = []
for n, (si, sj) in enumerate(SUPER):
    for a in range(2):
        for b in range(2):
            if 2 * si + a <= 2 * sj + b:
                PAIRS.append((2 * si + a, 2 * sj + b, n, a * PAD_K, b * PAD_K))
FIRST = [n for n in range(len(PAIRS)) if (n + 1) * ROWS <= PART]
HOPS = (0, 1, 2, 1)
PLANE = sorted(range(1, 16), key=lambda r: -HOPS[r // 4] - HOPS[r % 4])
RING = (2, 1, 3)
MESH = pl.DeviceIdType.MESH


def kernel(
    x, g, spread, drive_out, repel_out,
    xt, gt, xd, gd, acc, part, part_wire, from_core, core_sum, core_wire, from_y, y_sum, from_zx,
    kern, kern_wide, full, totals, product, drive_stage, repel_stage, drive_land, repel_land,
    x_send, x_recv, g_send, g_recv, d_send, d_recv, r_send, r_recv, own_sem,
    c_send, c_recv, y_send, y_recv, p_send, p_recv, ap_send, ap_recv, ay_send, ay_recv, ac_send, ac_recv,
):
    f32, bf16 = jnp.float32, jnp.bfloat16
    dom, feat = lax.axis_index("dom"), lax.axis_index("feat")
    z, x_lo = dom // 2, dom % 2
    y, x_hi, core = feat // 4, (feat // 2) % 2, feat % 2
    xx = x_hi * 2 + x_lo
    member = z * 4 + xx

    def dom_peer(r):
        return (z + r // 2) % 4 * 2 + (x_lo + r % 2) % 2

    def plane_peer(r):
        z2, x2 = (z + r // 4) % 4, (xx + r % 4) % 4
        return z2 * 4 + x2, (z2 * 2 + x2 % 2, y * 4 + x2 // 2 * 2 + core)

    def y_peer(r):
        y2 = (y + r) % 4
        return y2, (dom, y2 * 4 + x_hi * 2 + core)

    sibling = (dom, y * 4 + x_hi * 2 + 1 - core)

    barrier = pltpu.get_barrier_semaphore()

    for r in PLANE:
        pl.semaphore_signal(barrier, inc=1, device_id=plane_peer(r)[1], device_id_type=MESH)

    @pl.loop(1, 4)
    def _(r):
        pl.semaphore_signal(barrier, inc=1, device_id=y_peer(r)[1], device_id_type=MESH)

    pl.semaphore_signal(barrier, inc=1, device_id=sibling, device_id_type=MESH)
    pl.semaphore_wait(barrier, 19)

    def columns(block, c):
        return pl.ds(pl.multiple_of(block * WIDTH + c * PIECE, 128), PIECE)

    def remote(src, dst, send, recv, device):
        return pltpu.make_async_remote_copy(
            src_ref=src, dst_ref=dst, send_sem=send, recv_sem=recv, device_id=device, device_id_type=MESH)

    def all_of(ref, sem):
        pltpu.make_async_copy(ref, ref, sem).wait()

    def inward(src, dst, send, recv, start, width, r):
        to, c = dom_peer(r), start // PIECE
        source = src.at[:, pl.ds(pl.multiple_of(to * WIDTH + start, 128), width)]
        target = dst.at[c, dom, :, pl.ds(start % PIECE, width)]
        return remote(source, target, send.at[c], recv.at[c], (to, feat))

    def to_all(start_one):
        @pl.loop(0, BLOCKS - 1)
        def _(q):
            start_one(BLOCKS - 1 - q)

    def all_seven(slab, sem, c):
        all_of(slab.at[c, pl.ds(0, BLOCKS - 1)], sem.at[c])

    def start_x(c):
        to_all(lambda r: inward(x, xt, x_send, x_recv, c * PIECE, PIECE, r).start())

    def start_g(point):
        for p in range(sum(G_AT[:point]), sum(G_AT[: point + 1])):
            to_all(lambda r: inward(g, gt, g_send, g_recv, G_STARTS[p], G_WIDTHS[p], r).start())

    def own_copy(src, dst, which, c):
        return pltpu.make_async_copy(src.at[:, columns(dom, c)], dst.at[c, dom], own_sem.at[which, c])

    for c in range(PIECES):
        start_x(c)
    for c in range(PIECES):
        own_copy(x, xt, 0, c).start()
    for c in range(PIECES):
        own_copy(g, gt, 1, c).start()
    part[FLAT - 3 * PAD_K :] = jnp.zeros((3 * PAD_K, 128), f32)

    def spread_out(src, dst, c):
        @pl.loop(0, BLOCKS)
        def _(b):
            start = pl.multiple_of(b * PAD_K, PAD_K)
            dst[c, pl.ds(start + PAD_K - 32, 32)] = jnp.zeros((32, PIECE), bf16)
            dst[c, pl.ds(start, ROWS)] = src[c, b]

    for c in range(PIECES):
        all_seven(xt, x_send, c)
        if c > 0:
            start_g(c - 1)
        own_copy(x, xt, 0, c).wait()
        all_seven(xt, x_recv, c)
        spread_out(xt, xd, c)
        for n, (si, sj) in enumerate(SUPER):
            left = xd[c, si * 2 * PAD_K : (si + 1) * 2 * PAD_K]
            right = xd[c, sj * 2 * PAD_K : (sj + 1) * 2 * PAD_K]
            inner = lax.dot_general(left, right, (((1,), (1,)), ((), ())), preferred_element_type=f32)
            acc[n] = inner if c == 0 else acc[n] + inner

    size = (2 * PAD_K, 2 * PAD_K)
    on_diagonal = lax.broadcasted_iota(jnp.int32, size, 0) == lax.broadcasted_iota(jnp.int32, size, 1)
    sq_col, sq_row = [], []
    for n in range(4):
        picked = jnp.where(on_diagonal, acc[n], 0.0)
        col, row = jnp.sum(picked, axis=1, keepdims=True), jnp.sum(picked, axis=0, keepdims=True)
        for a in (0, PAD_K):
            sq_col.append(col[a : a + ROWS])
            sq_row.append(row[:, a : a + PAD_K])

    def to_core(h):
        rows = pl.ds(pl.multiple_of(h * PART + (1 - core) * HALF, 16), HALF)
        return remote(part_wire.at[rows], from_core.at[h], c_send.at[h], c_recv.at[h], sibling)

    for h in range(PARTS):
        for n, (a, b, s, row, lane) in enumerate(PAIRS):
            if (n in FIRST) == (h == 0) or (h == 0 and n == len(FIRST)):
                inner = acc[s, row : row + ROWS, lane : lane + PAD_K]
                part[n * ROWS : (n + 1) * ROWS] = sq_col[a] + sq_row[b] - 2.0 * inner
        rows = slice(h * PART, (h + 1) * PART)
        part_wire[rows] = part[rows].astype(bf16)
        to_core(h).start()
    start_g(2)

    def to_y(h, r):
        y2, device = y_peer(r)
        rows = pl.ds(pl.multiple_of(y2 * QUARTER, 16), QUARTER)
        return remote(core_wire.at[h, rows], from_y.at[h, r], y_send.at[h], y_recv.at[h], device)

    def to_plane(h, r):
        m2, device = plane_peer(r)
        rows = pl.ds(pl.multiple_of(m2 * CHUNK, 8), CHUNK)
        return remote(y_sum.at[h, rows], from_zx.at[h, r], p_send.at[h], p_recv.at[h], device)

    def mine(h):
        return pl.ds(pl.multiple_of(h * PART + core * HALF + y * QUARTER + member * CHUNK, 16), CHUNK)

    def kern_to_plane(h, r):
        rows = kern.at[mine(h)]
        return remote(rows, rows, ap_send.at[h], ap_recv.at[h], plane_peer(r)[1])

    def kern_to_y(h, r):
        rows = kern.at[pl.ds(pl.multiple_of(h * PART + core * HALF + y * QUARTER, 16), QUARTER)]
        return remote(rows, rows, ay_send.at[h, r], ay_recv.at[h, r], y_peer(r)[1])

    def kern_to_core(h, r):
        y2 = (y + 4 - r) % 4
        rows = kern.at[pl.ds(pl.multiple_of(h * PART + core * HALF + y2 * QUARTER, 16), QUARTER)]
        return remote(rows, rows, ac_send.at[h, r], ac_recv.at[h, r], sibling)

    for h in range(PARTS):
        to_core(h).wait_recv()
        rows = pl.ds(pl.multiple_of(h * PART + core * HALF, 16), HALF)
        core_sum[h] = part[rows] + from_core[h].astype(f32)
        core_wire[h] = core_sum[h].astype(bf16)
        for r in RING:
            to_y(h, r).start()
    for h in range(PARTS):
        all_of(from_y.at[h, pl.ds(1, 3)], y_recv.at[h])
        total = core_sum[h, pl.ds(pl.multiple_of(y * QUARTER, 16), QUARTER)]
        for r in range(1, 4):
            total = total + from_y[h, r].astype(f32)
        y_sum[h] = total

        for r in PLANE:
            to_plane(h, r).start()

        start_g(3 + h)

    width = DIMS * spread[0]
    for h in range(PARTS):
        from_zx[h, 0] = y_sum[h, pl.ds(pl.multiple_of(member * CHUNK, 8), CHUNK)]

        all_of(from_zx.at[h, pl.ds(1, 15)], p_recv.at[h])

        kern[mine(h)] = jnp.exp(-jnp.sum(from_zx[h], axis=0) / width).astype(bf16)

        for r in PLANE:
            kern_to_plane(h, r).start()

        start_g(5 + h)

    for h in range(PARTS):
        all_of(kern.at[pl.ds(0, 15 * CHUNK)], ap_recv.at[h])

        kern_to_core(h, 0).start()
        for r in RING:
            kern_to_y(h, r).start()
    for h in range(PARTS):
        for r in range(1, 4):
            kern_to_y(h, r).wait_recv()
            kern_to_core(h, r).start()

    real = lax.broadcasted_iota(jnp.int32, (PAD_K, PAD_K), 1) < ROWS
    for h in range(PARTS):
        for r in range(4):
            kern_to_core(h, r).wait_recv()
        rows = slice(h * PART, (h + 1) * PART)
        kern_wide[rows] = kern[rows].astype(f32)
        for n, (a, b, s, row, lane) in enumerate(PAIRS):
            if (n in FIRST) == (h == 0):
                block = kern_wide[n * ROWS : n * ROWS + PAD_K]
                square = jnp.where(real, block, 0.0)
                full[a * PAD_M : a * PAD_M + ROWS, b * PAD_K : (b + 1) * PAD_K] = square[:ROWS].astype(bf16)
                if a != b:
                    across = jnp.where(real, block.T, 0.0)
                    full[b * PAD_M : b * PAD_M + ROWS, a * PAD_K : (a + 1) * PAD_K] = across[:ROWS].astype(bf16)

    ones = jnp.ones((BLOCKS * PAD_K, PAD_K), bf16)
    totals[...] = jnp.dot(full[...], ones, preferred_element_type=f32)

    def outward(src, dst, send, recv, c, r):
        to = dom_peer(r)
        return remote(src.at[c, to], dst.at[c, dom], send.at[c], recv.at[c], (to, feat))

    def r_out(c, r):
        return outward(repel_stage, repel_land, r_send, r_recv, c, r)

    def d_out(c, r):
        return outward(drive_stage, drive_land, d_send, d_recv, c, r)

    def product_rows(i):
        return product[pl.ds(pl.multiple_of(i * PAD_M, 8), ROWS)]

    def repel_rows(c, i):
        here = xd[c, pl.ds(pl.multiple_of(i * PAD_K, 16), ROWS)].astype(f32)
        total = totals[pl.ds(pl.multiple_of(i * PAD_M, 8), ROWS)]
        return jnp.concatenate([total] * (PIECE // PAD_K), axis=1) * here - product_rows(i)

    @pl.loop(0, PIECES)
    def _(c):
        product[...] = jnp.dot(full[...], xd[c], preferred_element_type=f32)

        def one(r):
            i = dom_peer(r)
            repel_stage[c, i] = repel_rows(c, i).astype(bf16)
            r_out(c, r).start()

        to_all(one)

        repel_out[:, columns(dom, c)] = repel_rows(c, dom)

    for c in range(PIECES):
        own_copy(g, gt, 1, c).wait()

        all_seven(gt, g_recv, c)
        spread_out(gt, gd, c)

    @pl.loop(0, PIECES)
    def _(c):
        product[...] = jnp.dot(full[...], gd[c], preferred_element_type=f32)

        def one(r):
            i = dom_peer(r)
            drive_stage[c, i] = product_rows(i).astype(bf16)
            d_out(c, r).start()

        to_all(one)

        drive_out[:, columns(dom, c)] = product_rows(dom)

    for h in range(PARTS):
        to_core(h).wait_send()
        all_of(from_y.at[h, pl.ds(1, 3)], y_send.at[h])
        for r in range(1, 4):
            kern_to_y(h, r).wait_send()
        for r in range(4):
            kern_to_core(h, r).wait_send()

        all_of(from_zx.at[h, pl.ds(1, 15)], p_send.at[h])
        all_of(kern.at[pl.ds(0, 15 * CHUNK)], ap_send.at[h])

    for c in range(PIECES):
        all_seven(gt, g_send, c)

    def widen(land, out, send, recv):
        @pl.loop(0, PIECES)
        def _(c):
            all_seven(land, send, c)
            all_seven(land, recv, c)

            @pl.loop(1, BLOCKS)
            def _(k):
                source = (dom + k) % BLOCKS
                out[:, columns(source, c)] = land[c, source].astype(f32)

    widen(repel_land, repel_out, r_send, r_recv)
    widen(drive_land, drive_out, d_send, d_recv)


def per_device(particles, gradients, spread):
    bf16, f32 = jnp.bfloat16, jnp.float32
    vmem, dma = pltpu.VMEM, pltpu.SemaphoreType.DMA
    slab, dense = (PIECES, BLOCKS, ROWS, PIECE), (PIECES, BLOCKS * PAD_K, PIECE)
    drive, repel = pl.pallas_call(
        kernel,
        out_shape=[pltpu.VMEM((ROWS, COLS), f32)] * 2,
        in_specs=[pl.BlockSpec(memory_space=pl.ANY)] * 2 + [pl.BlockSpec(memory_space=pltpu.SMEM)],
        out_specs=[pl.BlockSpec(memory_space=pltpu.VMEM)] * 2,
        scratch_shapes=[
            vmem(slab, bf16), vmem(slab, bf16), vmem(dense, bf16), vmem(dense, bf16),
            vmem((len(SUPER), 2 * PAD_K, 2 * PAD_K), f32), vmem((FLAT, 128), f32), vmem((FLAT, 128), bf16),
            vmem((PARTS, HALF, 128), bf16), vmem((PARTS, HALF, 128), f32), vmem((PARTS, HALF, 128), bf16),
            vmem((PARTS, 4, QUARTER, 128), bf16), vmem((PARTS, QUARTER, 128), f32), vmem((PARTS, 16, CHUNK, 128), f32),
            vmem((FLAT, 128), bf16), vmem((FLAT, 128), f32), vmem((BLOCKS * PAD_M, BLOCKS * PAD_K), bf16),
            vmem((BLOCKS * PAD_M, PAD_K), f32), vmem((BLOCKS * PAD_M, PIECE), f32),
            vmem(slab, bf16), vmem(slab, bf16), vmem(slab, bf16), vmem(slab, bf16),
        ]
        + [dma((PIECES,))] * 8 + [dma((2, PIECES))]
        + [dma((PARTS,))] * 4
        + [dma((PARTS,))] * 4 + [dma((PARTS, 4))] * 4,
        compiler_params=pltpu.CompilerParams(
            collective_id=0, has_side_effects=True, vmem_limit_bytes=44 * 2**20),
        name="svgd",
    )(particles, gradients, spread)
    return drive, repel


def solution(mesh):
    return jax.shard_map(
        per_device,
        mesh=mesh,
        in_specs=(P("dom", "feat"), P("dom", "feat"), P()),
        out_specs=(P("dom", "feat"), P("dom", "feat")),
        check_vma=False,
    )
```

```python
import jax
import jax.numpy as jnp
from jax import lax
from jax.experimental import pallas as pl
from jax.experimental.pallas import tpu as pltpu
from jax.sharding import PartitionSpec as P

DIMS = 196608
ROWS = 104
PAD_K, PAD_M = 128, 112
COLS = 12288
BLOCKS = 8
PIECES = 2
WIDTH = COLS // BLOCKS
PIECE = WIDTH // PIECES
G_WIDTHS = (256, 256, 128, 128, 128, 128, 512)
G_STARTS = tuple(sum(G_WIDTHS[:p]) for p in range(len(G_WIDTHS)))
G_AT = (2, 0, 1, 0, 1, 1, 2)
PARTS = 2
FLAT = 4096
PART = FLAT // PARTS
HALF, QUARTER, CHUNK = PART // 2, PART // 8, PART // 128
SUPER = [(i, i) for i in range(4)] + [(i, j) for i in range(4) for j in range(i + 1, 4)]
PAIRS = []
for n, (si, sj) in enumerate(SUPER):
    for a in range(2):
        for b in range(2):
            if 2 * si + a <= 2 * sj + b:
                PAIRS.append((2 * si + a, 2 * sj + b, n, a * PAD_K, b * PAD_K))
FIRST = [n for n in range(len(PAIRS)) if (n + 1) * ROWS <= PART]
HOPS = (0, 1, 2, 1)
PLANE = sorted(range(1, 16), key=lambda r: -HOPS[r // 4] - HOPS[r % 4])
RING = (2, 1, 3)
MESH = pl.DeviceIdType.MESH


def kernel(
    x, g, spread, drive_out, repel_out,
    xt, gt, xd, gd, acc, part, part_wire, from_core, core_sum, core_wire, from_y, y_sum, from_zx,
    kern, kern_wide, full, totals, product, drive_stage, repel_stage, drive_land, repel_land,
    x_send, x_recv, g_send, g_recv, d_send, d_recv, r_send, r_recv, own_sem,
    c_send, c_recv, y_send, y_recv, p_send, p_recv, ap_send, ap_recv, ay_send, ay_recv, ac_send, ac_recv,
):
    f32, bf16 = jnp.float32, jnp.bfloat16
    dom, feat = lax.axis_index("dom"), lax.axis_index("feat")
    z, x_lo = dom // 2, dom % 2
    y, x_hi, core = feat // 4, (feat // 2) % 2, feat % 2
    xx = x_hi * 2 + x_lo
    member = z * 4 + xx

    def dom_peer(r):
        return (z + r // 2) % 4 * 2 + (x_lo + r % 2) % 2

    def plane_peer(r):
        z2, x2 = (z + r // 4) % 4, (xx + r % 4) % 4
        return z2 * 4 + x2, (z2 * 2 + x2 % 2, y * 4 + x2 // 2 * 2 + core)

    def y_peer(r):
        y2 = (y + r) % 4
        return y2, (dom, y2 * 4 + x_hi * 2 + core)

    sibling = (dom, y * 4 + x_hi * 2 + 1 - core)

    barrier = pltpu.get_barrier_semaphore()

    for r in PLANE:
        pl.semaphore_signal(barrier, inc=1, device_id=plane_peer(r)[1], device_id_type=MESH)

    @pl.loop(1, 4)
    def _(r):
        pl.semaphore_signal(barrier, inc=1, device_id=y_peer(r)[1], device_id_type=MESH)

    pl.semaphore_signal(barrier, inc=1, device_id=sibling, device_id_type=MESH)
    pl.semaphore_wait(barrier, 19)

    def columns(block, c):
        return pl.ds(pl.multiple_of(block * WIDTH + c * PIECE, 128), PIECE)

    def remote(src, dst, send, recv, device):
        return pltpu.make_async_remote_copy(
            src_ref=src, dst_ref=dst, send_sem=send, recv_sem=recv, device_id=device, device_id_type=MESH)

    def all_of(ref, sem):
        pltpu.make_async_copy(ref, ref, sem).wait()

    def inward(src, dst, send, recv, start, width, r):
        to, c = dom_peer(r), start // PIECE
        source = src.at[:, pl.ds(pl.multiple_of(to * WIDTH + start, 128), width)]
        target = dst.at[c, dom, :, pl.ds(start % PIECE, width)]
        return remote(source, target, send.at[c], recv.at[c], (to, feat))

    def to_all(start_one):
        @pl.loop(0, BLOCKS - 1)
        def _(q):
            start_one(BLOCKS - 1 - q)

    def all_seven(slab, sem, c):
        all_of(slab.at[c, pl.ds(0, BLOCKS - 1)], sem.at[c])

    def start_x(c):
        to_all(lambda r: inward(x, xt, x_send, x_recv, c * PIECE, PIECE, r).start())

    def start_g(point):
        for p in range(sum(G_AT[:point]), sum(G_AT[: point + 1])):
            to_all(lambda r: inward(g, gt, g_send, g_recv, G_STARTS[p], G_WIDTHS[p], r).start())

    def own_copy(src, dst, which, c):
        return pltpu.make_async_copy(src.at[:, columns(dom, c)], dst.at[c, dom], own_sem.at[which, c])

    for c in range(PIECES):
        start_x(c)
    for c in range(PIECES):
        own_copy(x, xt, 0, c).start()
    for c in range(PIECES):
        own_copy(g, gt, 1, c).start()
    part[FLAT - 3 * PAD_K :] = jnp.zeros((3 * PAD_K, 128), f32)

    def spread_out(src, dst, c):
        @pl.loop(0, BLOCKS)
        def _(b):
            start = pl.multiple_of(b * PAD_K, PAD_K)
            dst[c, pl.ds(start + PAD_K - 32, 32)] = jnp.zeros((32, PIECE), bf16)
            dst[c, pl.ds(start, ROWS)] = src[c, b]

    for c in range(PIECES):
        all_of(x.at[:, pl.ds(0, (BLOCKS - 1) * PIECE)], x_send.at[c])
        if c > 0:
            start_g(c - 1)
        own_copy(x, xt, 0, c).wait()
        all_seven(xt, x_recv, c)
        spread_out(xt, xd, c)
        for n, (si, sj) in enumerate(SUPER):
            left = xd[c, si * 2 * PAD_K : (si + 1) * 2 * PAD_K]
            right = xd[c, sj * 2 * PAD_K : (sj + 1) * 2 * PAD_K]
            inner = lax.dot_general(left, right, (((1,), (1,)), ((), ())), preferred_element_type=f32)
            acc[n] = inner if c == 0 else acc[n] + inner

    size = (2 * PAD_K, 2 * PAD_K)
    on_diagonal = lax.broadcasted_iota(jnp.int32, size, 0) == lax.broadcasted_iota(jnp.int32, size, 1)
    sq_col, sq_row = [], []
    for n in range(4):
        picked = jnp.where(on_diagonal, acc[n], 0.0)
        col, row = jnp.sum(picked, axis=1, keepdims=True), jnp.sum(picked, axis=0, keepdims=True)
        for a in (0, PAD_K):
            sq_col.append(col[a : a + ROWS])
            sq_row.append(row[:, a : a + PAD_K])

    def to_core(h):
        rows = pl.ds(pl.multiple_of(h * PART + (1 - core) * HALF, 16), HALF)
        return remote(part_wire.at[rows], from_core.at[h], c_send.at[h], c_recv.at[h], sibling)

    for h in range(PARTS):
        for n, (a, b, s, row, lane) in enumerate(PAIRS):
            if (n in FIRST) == (h == 0) or (h == 0 and n == len(FIRST)):
                inner = acc[s, row : row + ROWS, lane : lane + PAD_K]
                part[n * ROWS : (n + 1) * ROWS] = sq_col[a] + sq_row[b] - 2.0 * inner
        rows = slice(h * PART, (h + 1) * PART)
        part_wire[rows] = part[rows].astype(bf16)
        to_core(h).start()
    start_g(2)

    def to_y(h, r):
        y2, device = y_peer(r)
        rows = pl.ds(pl.multiple_of(y2 * QUARTER, 16), QUARTER)
        return remote(core_wire.at[h, rows], from_y.at[h, r], y_send.at[h], y_recv.at[h], device)

    def to_plane(h, r):
        m2, device = plane_peer(r)
        rows = pl.ds(pl.multiple_of(m2 * CHUNK, 8), CHUNK)
        return remote(y_sum.at[h, rows], from_zx.at[h, r], p_send.at[h], p_recv.at[h], device)

    def mine(h):
        return pl.ds(pl.multiple_of(h * PART + core * HALF + y * QUARTER + member * CHUNK, 16), CHUNK)

    def kern_to_plane(h, r):
        rows = kern.at[mine(h)]
        return remote(rows, rows, ap_send.at[h], ap_recv.at[h], plane_peer(r)[1])

    def kern_to_y(h, r):
        rows = kern.at[pl.ds(pl.multiple_of(h * PART + core * HALF + y * QUARTER, 16), QUARTER)]
        return remote(rows, rows, ay_send.at[h, r], ay_recv.at[h, r], y_peer(r)[1])

    def kern_to_core(h, r):
        y2 = (y + 4 - r) % 4
        rows = kern.at[pl.ds(pl.multiple_of(h * PART + core * HALF + y2 * QUARTER, 16), QUARTER)]
        return remote(rows, rows, ac_send.at[h, r], ac_recv.at[h, r], sibling)

    for h in range(PARTS):
        to_core(h).wait_recv()
        rows = pl.ds(pl.multiple_of(h * PART + core * HALF, 16), HALF)
        core_sum[h] = part[rows] + from_core[h].astype(f32)
        core_wire[h] = core_sum[h].astype(bf16)
        for r in RING:
            to_y(h, r).start()
    for h in range(PARTS):
        all_of(from_y.at[h, pl.ds(1, 3)], y_recv.at[h])
        total = core_sum[h, pl.ds(pl.multiple_of(y * QUARTER, 16), QUARTER)]
        for r in range(1, 4):
            total = total + from_y[h, r].astype(f32)
        y_sum[h] = total

        for r in PLANE:
            to_plane(h, r).start()

        start_g(3 + h)

    width = DIMS * spread[0]
    for h in range(PARTS):
        from_zx[h, 0] = y_sum[h, pl.ds(pl.multiple_of(member * CHUNK, 8), CHUNK)]

        all_of(from_zx.at[h, pl.ds(1, 15)], p_recv.at[h])

        kern[mine(h)] = jnp.exp(-jnp.sum(from_zx[h], axis=0) / width).astype(bf16)

        for r in PLANE:
            kern_to_plane(h, r).start()

        start_g(5 + h)

    for h in range(PARTS):
        all_of(kern.at[pl.ds(0, 15 * CHUNK)], ap_recv.at[h])

        kern_to_core(h, 0).start()
        for r in RING:
            kern_to_y(h, r).start()
    for h in range(PARTS):
        for r in range(1, 4):
            kern_to_y(h, r).wait_recv()
            kern_to_core(h, r).start()

    real = lax.broadcasted_iota(jnp.int32, (PAD_K, PAD_K), 1) < ROWS
    for h in range(PARTS):
        for r in range(4):
            kern_to_core(h, r).wait_recv()
        rows = slice(h * PART, (h + 1) * PART)
        kern_wide[rows] = kern[rows].astype(f32)
        for n, (a, b, s, row, lane) in enumerate(PAIRS):
            if (n in FIRST) == (h == 0):
                block = kern_wide[n * ROWS : n * ROWS + PAD_K]
                square = jnp.where(real, block, 0.0)
                full[a * PAD_M : a * PAD_M + ROWS, b * PAD_K : (b + 1) * PAD_K] = square[:ROWS].astype(bf16)
                if a != b:
                    across = jnp.where(real, block.T, 0.0)
                    full[b * PAD_M : b * PAD_M + ROWS, a * PAD_K : (a + 1) * PAD_K] = across[:ROWS].astype(bf16)

    ones = jnp.ones((BLOCKS * PAD_K, PAD_K), bf16)
    totals[...] = jnp.dot(full[...], ones, preferred_element_type=f32)

    def outward(src, dst, send, recv, c, r):
        to = dom_peer(r)
        return remote(src.at[c, to], dst.at[c, dom], send.at[c], recv.at[c], (to, feat))

    def r_out(c, r):
        return outward(repel_stage, repel_land, r_send, r_recv, c, r)

    def d_out(c, r):
        return outward(drive_stage, drive_land, d_send, d_recv, c, r)

    def product_rows(i):
        return product[pl.ds(pl.multiple_of(i * PAD_M, 8), ROWS)]

    def repel_rows(c, i):
        here = xd[c, pl.ds(pl.multiple_of(i * PAD_K, 16), ROWS)].astype(f32)
        total = totals[pl.ds(pl.multiple_of(i * PAD_M, 8), ROWS)]
        return jnp.concatenate([total] * (PIECE // PAD_K), axis=1) * here - product_rows(i)

    @pl.loop(0, PIECES)
    def _(c):
        product[...] = jnp.dot(full[...], xd[c], preferred_element_type=f32)

        def one(r):
            i = dom_peer(r)
            repel_stage[c, i] = repel_rows(c, i).astype(bf16)
            r_out(c, r).start()

        to_all(one)

        repel_out[:, columns(dom, c)] = repel_rows(c, dom)

    for c in range(PIECES):
        own_copy(g, gt, 1, c).wait()

        all_seven(gt, g_recv, c)
        spread_out(gt, gd, c)

    @pl.loop(0, PIECES)
    def _(c):
        product[...] = jnp.dot(full[...], gd[c], preferred_element_type=f32)

        def one(r):
            i = dom_peer(r)
            drive_stage[c, i] = product_rows(i).astype(bf16)
            d_out(c, r).start()

        to_all(one)

        drive_out[:, columns(dom, c)] = product_rows(dom)

    for h in range(PARTS):
        to_core(h).wait_send()
        all_of(from_y.at[h, pl.ds(1, 3)], y_send.at[h])
        for r in range(1, 4):
            kern_to_y(h, r).wait_send()
        for r in range(4):
            kern_to_core(h, r).wait_send()

        all_of(from_zx.at[h, pl.ds(1, 15)], p_send.at[h])
        all_of(kern.at[pl.ds(0, 15 * CHUNK)], ap_send.at[h])

    for c in range(PIECES):
        all_of(g.at[:, pl.ds(0, (BLOCKS - 1) * PIECE)], g_send.at[c])

    def widen(land, out, send, recv):
        @pl.loop(0, PIECES)
        def _(c):
            all_seven(land, send, c)
            all_seven(land, recv, c)

            @pl.loop(1, BLOCKS)
            def _(k):
                source = (dom + k) % BLOCKS
                out[:, columns(source, c)] = land[c, source].astype(f32)

    widen(repel_land, repel_out, r_send, r_recv)
    widen(drive_land, drive_out, d_send, d_recv)


def per_device(particles, gradients, spread):
    bf16, f32 = jnp.bfloat16, jnp.float32
    vmem, dma = pltpu.VMEM, pltpu.SemaphoreType.DMA
    slab, dense = (PIECES, BLOCKS, ROWS, PIECE), (PIECES, BLOCKS * PAD_K, PIECE)
    drive, repel = pl.pallas_call(
        kernel,
        out_shape=[pltpu.VMEM((ROWS, COLS), f32)] * 2,
        in_specs=[pl.BlockSpec(memory_space=pl.ANY)] * 2 + [pl.BlockSpec(memory_space=pltpu.SMEM)],
        out_specs=[pl.BlockSpec(memory_space=pltpu.VMEM)] * 2,
        scratch_shapes=[
            vmem(slab, bf16), vmem(slab, bf16), vmem(dense, bf16), vmem(dense, bf16),
            vmem((len(SUPER), 2 * PAD_K, 2 * PAD_K), f32), vmem((FLAT, 128), f32), vmem((FLAT, 128), bf16),
            vmem((PARTS, HALF, 128), bf16), vmem((PARTS, HALF, 128), f32), vmem((PARTS, HALF, 128), bf16),
            vmem((PARTS, 4, QUARTER, 128), bf16), vmem((PARTS, QUARTER, 128), f32), vmem((PARTS, 16, CHUNK, 128), f32),
            vmem((FLAT, 128), bf16), vmem((FLAT, 128), f32), vmem((BLOCKS * PAD_M, BLOCKS * PAD_K), bf16),
            vmem((BLOCKS * PAD_M, PAD_K), f32), vmem((BLOCKS * PAD_M, PIECE), f32),
            vmem(slab, bf16), vmem(slab, bf16), vmem(slab, bf16), vmem(slab, bf16),
        ]
        + [dma((PIECES,))] * 8 + [dma((2, PIECES))]
        + [dma((PARTS,))] * 4
        + [dma((PARTS,))] * 4 + [dma((PARTS, 4))] * 4,
        compiler_params=pltpu.CompilerParams(
            collective_id=0, has_side_effects=True, vmem_limit_bytes=44 * 2**20),
        name="svgd",
    )(particles, gradients, spread)
    return drive, repel


def solution(mesh):
    return jax.shard_map(
        per_device,
        mesh=mesh,
        in_specs=(P("dom", "feat"), P("dom", "feat"), P()),
        out_specs=(P("dom", "feat"), P("dom", "feat")),
        check_vma=False,
    )
```
